1024 devices in a mesh: dp: 4 (over z_hi, core), ctx: 32 (over x, z_lo), tensor: 8 (over y).
Axes of the slice: x: 8, y: 8, z: 8 (z_hi: 2, z_lo: 4; z = z_hi * 4 + z_lo), core: 2. Of those that a mesh axis runs over, the one named last changes fastest.
Arguments:
- out_grad: bfloat16 [4, 8192, 4096], P('dp', ('ctx', 'tensor')), may hold values from -1 to 1
- prev_state: bfloat16 [4, 8192, 4096], P('dp', 'ctx', 'tensor'), may hold values from -6 to 6
- boundary: int32 [4, 8192], P('dp', 'ctx'), may hold values 0 or 1
- angle_code: int32 [64, 32], P('tensor'), may hold values from 0 to 4095
- radius_code: int32 [64, 32], P('tensor'), may hold values from 0 to 1023
- reflect: float32 [64, 4, 64], P('tensor'), may hold values from -6 to 6
Outputs:
- grad_input: bfloat16 [4, 8192, 4096], P('dp', 'ctx', 'tensor')
- grad_transition: float32 [64, 64, 64], P('tensor')
The draws below stay inside these ranges and needn't reach their ends.
All inputs are finite; a program needn't handle non-finite values. No bound on the sum of `boundary` on one device may be relied on, other than what follows from the above.
Results may differ from the reference program's by a relative error of at most 0.003.
Values may be sent and summed in bfloat16 or wider, within the bound.
A program may use at most 64 MiB of HBM per device.

```python
import math
import jax
import jax.numpy as jnp
from jax import lax

BLOCKS = 64
BSIZE = 64
TOK_DEV = 256
WIDTH = 4096
SEQLEN = 8192
NSEQ = 4
N_CTX = 32


def touch_ends(values, rng, least, largest):
    longest = values.shape.index(max(values.shape))
    spots = []
    for shift in (0, 1):
        where = [jax.random.randint(jax.random.fold_in(rng, axis), (), 0, length) for axis, length in enumerate(values.shape)]
        where[longest] = (where[longest] + shift) % values.shape[longest]
        spots.append(tuple(where))
    return values.at[spots[0]].set(least).at[spots[1]].set(largest)


def steps_of(stream_key, dims, pieces, least, high):
    factor_of, own = 1.0, jax.random.fold_in(stream_key, 6)
    for position, parts in pieces:
        draws = jnp.exp(jax.random.uniform(jax.random.fold_in(own, position), (parts,), jnp.float32, least / len(pieces), high / len(pieces)))
        factor_of = factor_of * jnp.repeat(draws, dims[position] // parts).reshape([-1 if axis == position else 1 for axis in range(len(dims))])
    return factor_of


def normal_values(stream_key, extent, deviation, bound, pieces=(), kind=jnp.bfloat16):
    level = steps_of(stream_key, extent, pieces, -0.22, 0.18) if pieces else 1.0
    entries = jax.random.normal(stream_key, extent, jnp.float32) * deviation * level
    return jnp.minimum(jnp.maximum(entries, -bound), bound).astype(kind)


def setup_inputs(seed: int = 0) -> dict:
    key_list = jax.random.split(jax.random.key(seed), 7)
    out_grad = normal_values(key_list[0], (NSEQ, SEQLEN, WIDTH), 0.125, 1.0, ((0, 4), (1, 256)))
    prev_state = normal_values(key_list[1], (NSEQ, SEQLEN, WIDTH), 1.0, 6.0, ((0, 4), (1, 32), (2, 8)))
    boundary = touch_ends((jax.random.randint(key_list[2], (NSEQ, SEQLEN), 0, TOK_DEV * N_CTX // 4) < 1).astype(jnp.int32), jax.random.fold_in(key_list[2], 1), 0, 1)
    angle_code = touch_ends(jax.random.randint(key_list[3], (BLOCKS, BSIZE // 2), 0, 4096), jax.random.fold_in(key_list[3], 1), 0, 4095).astype(jnp.int32)
    radius_code = touch_ends(jax.random.randint(key_list[4], (BLOCKS, BSIZE // 2), 0, 1024), jax.random.fold_in(key_list[4], 1), 0, 1023).astype(jnp.int32)
    reflect = normal_values(key_list[5], (BLOCKS, 4, BSIZE), 1.0, 6.0, ((0, 8),), jnp.float32)
    return dict(out_grad=out_grad, prev_state=prev_state, boundary=boundary, angle_code=angle_code, radius_code=radius_code, reflect=reflect)


def transition(angle_code, radius_code, reflect):
    block_count = radius_code.shape[0]
    block_size = 2 * radius_code.shape[1]
    rates = jnp.exp2(-(4.0 + radius_code.astype(jnp.float32) * (10.0 / 1024.0)))
    radius = 1.0 - rates
    angles = angle_code.astype(jnp.float32) * (math.pi / 4096.0)
    cosine = jnp.repeat(radius * jnp.cos(angles), 2, axis=1)[:, :, None]
    sine_part = jnp.repeat(radius * jnp.sin(angles), 2, axis=1)[:, :, None]
    row_index = jnp.arange(block_size)[:, None]
    col_index = jnp.arange(block_size)[None, :]
    on_diagonal = row_index == col_index
    upper_pair = (row_index % 2 == 0) & (col_index == row_index + 1)
    lower_pair = (row_index % 2 == 1) & (col_index == row_index - 1)
    zero_value = jnp.float32(0.0)
    rotation = jnp.where(on_diagonal[None], cosine, zero_value) + jnp.where(upper_pair[None], -sine_part, zero_value) + jnp.where(lower_pair[None], sine_part, zero_value)
    basis_now = jnp.broadcast_to(jnp.eye(block_size, dtype=jnp.float32), (block_count, block_size, block_size))
    for reflect_index in range(4):
        reflector = reflect[:, reflect_index, :].astype(jnp.float32)
        norm_sq = jnp.sum(reflector * reflector, axis=1)
        projected = jnp.einsum('bij,bj->bi', basis_now, reflector, precision=lax.Precision.HIGHEST)
        basis_now = basis_now - 2.0 * projected[:, :, None] * reflector[:, None, :] / norm_sq[:, None, None]
    rotated = jnp.einsum('bij,bjk->bik', basis_now, rotation, precision=lax.Precision.HIGHEST)
    return jnp.einsum('bik,blk->bil', rotated, basis_now, precision=lax.Precision.HIGHEST)


def reference(out_grad, prev_state, boundary, angle_code, radius_code, reflect):
    transit = transition(angle_code, radius_code, reflect)
    sequences, length, width_all = out_grad.shape
    grad_rows = out_grad.astype(jnp.float32).reshape(sequences, length, BLOCKS, BSIZE)
    previous = prev_state.astype(jnp.float32).reshape(sequences, length, BLOCKS, BSIZE)
    retain = jnp.where(boundary == 1, jnp.float32(0.6), jnp.float32(1.0)).astype(jnp.float32)

    def advance(state_pair, inputs):
        adjoint_next, accumulated = state_pair
        grad_row, prev_row, keep_row = inputs
        adjoint = grad_row + keep_row[:, None, None] * jnp.einsum('bji,sbj->sbi', transit, adjoint_next, precision=lax.Precision.HIGHEST)
        accumulated = accumulated + jnp.einsum('sbi,sbj->bij', adjoint, prev_row, precision=lax.Precision.HIGHEST)
        return (adjoint, accumulated), adjoint.astype(jnp.bfloat16)

    initial = (jnp.zeros((sequences, BLOCKS, BSIZE), jnp.float32), jnp.zeros((BLOCKS, BSIZE, BSIZE), jnp.float32))
    sequence_inputs = (jnp.swapaxes(grad_rows, 0, 1), jnp.swapaxes(previous, 0, 1), jnp.swapaxes(retain, 0, 1))
    (final_adjoint, grad_transition), outputs = lax.scan(advance, initial, sequence_inputs, reverse=True)
    grad_input = jnp.swapaxes(outputs, 0, 1).reshape(sequences, length, width_all)
    return grad_input, grad_transition
```

```python
import functools
import math

import jax
import jax.numpy as jnp
from jax import lax
from jax.experimental import pallas as pl
from jax.experimental.pallas import tpu as pltpu
from jax.sharding import Mesh
from jax.sharding import PartitionSpec as P

F32, BF16, I32 = jnp.float32, jnp.bfloat16, jnp.int32
NN = (((1,), (0,)), ((), ()))
NT = (((1,), (1,)), ((), ()))
TN = (((0,), (0,)), ((), ()))
MESH = pl.DeviceIdType.MESH

TOK, CH, SUB, STEP = 256, 512, 8, 32
BS, NB = 64, 8
DP = ("zh", "core")
CTX = ("x", "zl")


def iota(shape, axis):
    return lax.broadcasted_iota(I32, shape, axis)


def dot(a, b, dims):
    return lax.dot_general(a, b, dims, preferred_element_type=F32)


def fdot(a, b, dims):
    return lax.dot_general(a, b, dims, precision=lax.Precision.HIGHEST, preferred_element_type=F32)


def split(a):
    hi = a.astype(BF16)
    return hi, (a - hi.astype(F32)).astype(BF16)


def cmul(a, b):
    return a[0] * b[0] - a[1] * b[1], a[0] * b[1] + a[1] * b[0]


def cadd(a, b):
    return a[0] + b[0], a[1] + b[1]


def cwhere(m, a, b):
    return jnp.where(m, a[0], b[0]), jnp.where(m, a[1], b[1])


def compact(full):
    lane_block = (iota((BS, 256), 1) % 128) // 32
    out = jnp.zeros((BS, 256), F32)
    for bb in range(4):
        out = jnp.where(lane_block == bb, full[BS * bb : BS * bb + BS], out)
    return out


def kernel(
    sizes, og, ps, bd, ac, rc, rf, gi, gt,
    g, pv, whi, wlo, kl, wq, un, cn, qc, gc, gr, bz, bx, gsum, rcore, rx, rz,
    lsem, ysend, yrecv, bzs, bzr, bxs, bxr, css, csr, xss, xsr, zss, zsr, xas, xar, cas, car,
):
    n_zh, n_core, n_x, n_zl, n_y = sizes
    n_z = n_zh * n_zl
    zh, core, x, zl, y = (lax.axis_index(a) for a in ("zh", "core", "x", "zl", "y"))
    z = zh * n_zl + zl
    rows = TOK // n_y

    def at_y(d):
        return {"y": lax.rem(y + d, n_y)}

    def at_x(d):
        return {"x": lax.rem(x + d, n_x)}

    def at_z(d):
        k = lax.rem(z + d, n_z)
        return {"zh": k // n_zl, "zl": lax.rem(k, n_zl)}

    def at_zl(d):
        return {"zl": lax.rem(zl + d, n_zl)}

    sibling = {"core": 1 - core}
    partners = (
        [at_y(d) for d in range(1, n_y)]
        + [at_x(d) for d in range(1, n_x)]
        + [at_z(d) for d in range(1, n_z)]
        + [sibling]
    )
    barrier = pltpu.get_barrier_semaphore()
    for partner in partners:
        pl.semaphore_signal(barrier, inc=1, device_id=partner, device_id_type=MESH)

    def remote(src, dst, send, recv, where):
        return pltpu.make_async_remote_copy(
            src_ref=src, dst_ref=dst, send_sem=send, recv_sem=recv, device_id=where, device_id_type=MESH
        )

    load_prev = pltpu.make_async_copy(ps.at[0], pv, lsem.at[0])
    load_prev.start()
    own_rows = pl.ds(pl.multiple_of(y * rows, rows), rows)
    load_own = pltpu.make_async_copy(
        og.at[0, :, pl.ds(pl.multiple_of(y * CH, CH), CH)], g.at[own_rows], lsem.at[1]
    )
    load_own.start()
    pl.semaphore_wait(barrier, len(partners))

    a2a = []
    for d in range(1, n_y):
        k = lax.rem(y + d, n_y)
        a2a.append(
            remote(
                og.at[0, :, pl.ds(pl.multiple_of(k * CH, CH), CH)],
                g.at[own_rows], ysend.at[d], yrecv.at[d], {"y": k},
            )
        )
        a2a[-1].start()

    pick = (iota((32, 128), 1) % 32 == iota((32, 128), 0)).astype(F32)
    acode = fdot(ac[...].astype(F32), pick, NN)
    rcode = fdot(rc[...].astype(F32), pick, NN)
    radius = 1.0 - jnp.exp2(-(4.0 + rcode * (10.0 / 1024.0)))
    angle = acode * (math.pi / 4096.0)
    lam_r, lam_i = radius * jnp.cos(angle), -radius * jnp.sin(angle)
    lam = []
    for h in range(2):
        mine = iota((NB, 128), 0) == 4 * h + iota((NB, 128), 1) // 32
        lam.append(
            tuple(
                jnp.broadcast_to(jnp.sum(jnp.where(mine, v, 0.0), axis=0, keepdims=True), (SUB, 128))
                for v in (lam_r, lam_i)
            )
        )

    r_id, t_id = iota((TOK, TOK), 0), iota((TOK, TOK), 1)
    chosen = t_id == (r_id % SUB) * STEP + r_id // SUB
    marks = jnp.where(chosen & (bd[...] == 1), 1.0, 0.0).astype(BF16)
    keep = jnp.where(dot(marks, jnp.ones((TOK, 128), BF16), NN) > 0.5, F32(0.6), F32(1.0))
    for h in range(2):
        for part in range(2):
            kl[2 * h + part] = keep * lam[h][part][0:1]

    lane = iota((BS, 256), 1)
    spread = (iota((NB, 256), 1) // 32 == iota((NB, 256), 0)).astype(F32)
    xs = [(iota((BS, 256), 0) == 2 * (lane % 32) + part).astype(F32) for part in range(2)]
    for k in (3, 2, 1, 0):
        v = fdot(rf[:, k, :], spread, TN)
        scale = 2.0 / jnp.sum(v * v, axis=0, keepdims=True)
        xs = [m - v * (scale * jnp.sum(v * m, axis=0, keepdims=True)) for m in xs]
    lane_block = (lane % 128) // 32
    for h in range(2):
        half = jnp.concatenate([m[:, 128 * h : 128 * h + 128] for m in xs], axis=1)
        for bb in range(4):
            hi, lo = split(jnp.where(lane_block == bb, half, 0.0))
            whi[h, BS * bb : BS * bb + BS, :] = hi
            wlo[h, BS * bb : BS * bb + BS, :] = lo

    def at_q(ref, q):
        return [(ref[2 * h, pl.ds(q * SUB, SUB), :], ref[2 * h + 1, pl.ds(q * SUB, SUB), :]) for h in range(2)]

    def at_t(ref, q):
        return [
            (ref[2 * h, pl.ds(q, SUB, stride=STEP), :], ref[2 * h + 1, pl.ds(q, SUB, stride=STEP), :])
            for h in range(2)
        ]

    def put_t(ref, q, value):
        for h in range(2):
            for part in range(2):
                ref[2 * h + part, pl.ds(q, SUB, stride=STEP), :] = value[h][part]

    def weights(i, w):
        for u in range(4):
            q = STEP - 1 - (4 * i + u)
            w = [cmul(a, b) for a, b in zip(at_q(kl, q), w)]
            for h in range(2):
                for part in range(2):
                    wq[2 * h + part, pl.ds(q * SUB, SUB), :] = w[h][part]
        return w

    one = (jnp.ones((SUB, 128), F32), jnp.zeros((SUB, 128), F32))
    m1 = lax.fori_loop(0, STEP // 4, weights, [one, one])
    sub = iota((SUB, 128), 0)

    def later(v, m):
        return tuple(pltpu.roll(p, SUB - m, 0) for p in v)

    zero = (jnp.zeros((SUB, 128), F32), jnp.zeros((SUB, 128), F32))
    hops, base = [], []
    for h in range(2):
        steps = [cwhere(sub < SUB - 1, m1[h], zero)]
        b = cwhere(sub < SUB - 1, later(m1[h], 1), one)
        for m in (1, 2, 4):
            if m > 1:
                steps.append(cmul(steps[-1], later(steps[-1], m // 2)))
            b = cmul(b, cwhere(sub < SUB - m, later(b, m), one))
        hops.append(steps)
        base.append(b)

    def enter(i, _):
        for u in range(4):
            q = 4 * i + u
            put_t(un, q, [cmul(a, b) for a, b in zip(at_q(wq, q), base)])
        return 0

    lax.fori_loop(0, STEP // 4, enter, 0)
    mu = [(un[2 * h, 0:1, :], un[2 * h + 1, 0:1, :]) for h in range(2)]

    def with_prev(ref, h):
        prev = pv[:, 256 * h : 256 * h + 256]
        hi, lo = split(jnp.concatenate([ref[2 * h], ref[2 * h + 1]], axis=1))
        return compact(dot(prev, hi, TN) + dot(prev, lo, TN))

    load_prev.wait()
    for h in range(2):
        qc[:, 256 * h : 256 * h + 256] = with_prev(un, h)

    load_own.wait()
    for copy in a2a:
        copy.wait_recv()
    for h in range(2):
        rows_h = g[:, 256 * h : 256 * h + 256]
        turned = dot(rows_h, whi[h], NN) + dot(rows_h, wlo[h], NN)
        cn[2 * h] = turned[:, :128]
        cn[2 * h + 1] = turned[:, 128:]

    def back(i, c):
        for u in range(4):
            q = STEP - 1 - (4 * i + u)
            c = [cadd(a, cmul(b, v)) for a, b, v in zip(at_t(cn, q), at_q(kl, q), c)]
            put_t(cn, q, c)
        return c

    first = lax.fori_loop(0, STEP // 4, back, [zero, zero])
    entering = []
    for h in range(2):
        v = first[h]
        for m, step in zip((1, 2, 4), hops[h]):
            v = cadd(v, cmul(step, later(v, m)))
        entering.append(cwhere(sub < SUB - 1, later(v, 1), zero))
        for part in range(2):
            bz[zl, 2 * part + h : 2 * part + h + 1, :] = v[part][0:1]
            bz[zl, 4 + 2 * part + h : 5 + 2 * part + h, :] = mu[h][part]

    zcopies = [remote(bz.at[zl], bz.at[zl], bzs.at[d], bzr.at[d], at_zl(d)) for d in range(1, n_zl)]
    for copy in zcopies:
        copy.start()

    def fix(i, _):
        for u in range(4):
            q = 4 * i + u
            put_t(cn, q, [cadd(a, cmul(b, v)) for a, b, v in zip(at_t(cn, q), at_q(wq, q), entering)])
        return 0

    lax.fori_loop(0, STEP // 4, fix, 0)
    for copy in zcopies:
        copy.wait_recv()

    def firsts(ref, j):
        return ((ref[j, 0:2, :], ref[j, 2:4, :]), (ref[j, 4:6, :], ref[j, 6:8, :]))

    zero2 = (jnp.zeros((2, 128), F32), jnp.zeros((2, 128), F32))
    one2 = (jnp.ones((2, 128), F32), jnp.zeros((2, 128), F32))

    def chain(ref, count, me):
        inside, passing = zero2, one2
        total, span = zero2, one2
        for j in reversed(range(count)):
            f, m = firsts(ref, j)
            total, span = cadd(f, cmul(m, total)), cmul(m, span)
            inside = cwhere(j > me, total, inside)
            passing = cwhere(j > me, span, passing)
        return inside, passing, total, span

    inside, passing, total, span = chain(bz, n_zl, zl)
    for part in range(2):
        bx[x, 2 * part : 2 * part + 2, :] = total[part]
        bx[x, 4 + 2 * part : 6 + 2 * part, :] = span[part]
    xcopies = [remote(bx.at[x], bx.at[x], bxs.at[d], bxr.at[d], at_x(d)) for d in range(1, n_x)]
    for copy in xcopies:
        copy.start()
    for h in range(2):
        gc[:, 256 * h : 256 * h + 256] = with_prev(cn, h)
    for copy in xcopies:
        copy.wait_recv()
    beyond, _, _, _ = chain(bx, n_x, x)
    entry = cadd(inside, cmul(passing, beyond))
    for h in range(2):
        e = (entry[0][h : h + 1], entry[1][h : h + 1])
        lo, hi = slice(256 * h, 256 * h + 128), slice(256 * h + 128, 256 * h + 256)
        add = cmul(e, (qc[:, lo], qc[:, hi]))
        gc[:, lo] += add[0]
        gc[:, hi] += add[1]

    def half(k):
        return pl.ds(pl.multiple_of(k * 256, 256), 256)

    def slab(k):
        return pl.ds(pl.multiple_of(k * (BS // n_x), BS // n_x), BS // n_x)

    to_core = remote(gc.at[:, half(1 - core)], rcore, css.at[0], csr.at[0], sibling)
    to_core.start()

    for h in range(2):
        e = (entry[0][h : h + 1], entry[1][h : h + 1])
        c = cadd((cn[2 * h], cn[2 * h + 1]), cmul(e, (un[2 * h], un[2 * h + 1])))
        hi, lo = split(jnp.concatenate(c, axis=1))
        adj = dot(hi, whi[h], NT) + dot(lo, whi[h], NT) + dot(hi, wlo[h], NT)
        gi[0, :, 256 * h : 256 * h + 256] = adj.astype(BF16)

    to_core.wait_recv()
    gsum[...] = gc[:, half(core)] + rcore[...]
    to_x = []
    for d in range(1, n_x):
        k = lax.rem(x + d, n_x)
        to_x.append(remote(gsum.at[slab(k)], rx.at[x], xss.at[d], xsr.at[d], {"x": k}))
        to_x[-1].start()
    rx[x] = gsum[slab(x), :]
    for copy in to_x:
        copy.wait_recv()
    rz[z] = jnp.sum(rx[...], axis=0)
    to_z = [remote(rz.at[z], rz.at[z], zss.at[d], zsr.at[d], at_z(d)) for d in range(1, n_z)]
    for copy in to_z:
        copy.start()
    for copy in to_z:
        copy.wait_recv()
    gr[slab(x), half(core)] = jnp.sum(rz[...], axis=0)
    mine = gr.at[slab(x), half(core)]
    back_x = [remote(mine, mine, xas.at[d], xar.at[d], at_x(d)) for d in range(1, n_x)]
    for copy in back_x:
        copy.start()
    for copy in back_x:
        copy.wait_recv()
    ours = gr.at[:, half(core)]
    back_core = remote(ours, ours, cas.at[0], car.at[0], sibling)
    back_core.start()
    back_core.wait_recv()
    for h in range(2):
        hi, lo = split(gr[:, 256 * h : 256 * h + 256])
        out = dot(whi[h], hi, NT) + dot(whi[h], lo, NT) + dot(wlo[h], hi, NT)
        gt[4 * h : 4 * h + 4] = out.reshape(4, BS, BS)

    for copy in a2a + zcopies + xcopies + to_x + to_z + back_x + [to_core, back_core]:
        copy.wait_send()


def body(sizes, out_grad, prev_state, boundary, angle_code, radius_code, reflect):
    n_zh, n_core, n_x, n_zl, n_y = sizes
    n_z = n_zh * n_zl
    slab = BS // n_x
    vmem, anywhere = pl.BlockSpec(memory_space=pltpu.VMEM), pl.BlockSpec(memory_space=pl.ANY)
    plane = pltpu.VMEM((4, TOK, 128), F32)
    dma = pltpu.SemaphoreType.DMA
    return pl.pallas_call(
        functools.partial(kernel, sizes),
        out_shape=(
            jax.ShapeDtypeStruct((1, TOK, CH), BF16),
            jax.ShapeDtypeStruct((NB, BS, BS), F32),
        ),
        in_specs=[anywhere, anywhere, vmem, vmem, vmem, vmem],
        out_specs=(vmem, vmem),
        scratch_shapes=[
            pltpu.VMEM((TOK, CH), BF16),
            pltpu.VMEM((TOK, CH), BF16),
            pltpu.VMEM((2, 256, 256), BF16),
            pltpu.VMEM((2, 256, 256), BF16),
            plane, plane, plane, plane,
            pltpu.VMEM((BS, CH), F32),
            pltpu.VMEM((BS, CH), F32),
            pltpu.VMEM((BS, CH), F32),
            pltpu.VMEM((n_zl, 8, 128), F32),
            pltpu.VMEM((n_x, 8, 128), F32),
            pltpu.VMEM((BS, 256), F32),
            pltpu.VMEM((BS, 256), F32),
            pltpu.VMEM((n_x, slab, 256), F32),
            pltpu.VMEM((n_z, slab, 256), F32),
            dma((2,)),
            dma((n_y,)), dma((n_y,)),
            dma((n_zl,)), dma((n_zl,)),
            dma((n_x,)), dma((n_x,)),
            dma((1,)), dma((1,)),
            dma((n_x,)), dma((n_x,)),
            dma((n_z,)), dma((n_z,)),
            dma((n_x,)), dma((n_x,)),
            dma((1,)), dma((1,)),
        ],
        compiler_params=pltpu.CompilerParams(
            collective_id=0, has_side_effects=True, vmem_limit_bytes=32 * 2**20
        ),
    )(out_grad, prev_state, boundary, angle_code, radius_code, reflect)


def solution(mesh):
    n_dp, n_ctx, n_y = (mesh.shape[a] for a in ("dp", "ctx", "tensor"))
    n_x = min(8, n_ctx // 2)
    sizes = (n_dp // 2, 2, n_x, n_ctx // n_x, n_y)
    fine = Mesh(mesh.devices.reshape(sizes), ("zh", "core", "x", "zl", "y"))
    in_specs = (
        P(DP, (*CTX, "y"), None),
        P(DP, CTX, "y"),
        P(DP, CTX),
        P("y", None),
        P("y", None),
        P("y", None, None),
    )
    out_specs = (P(DP, CTX, "y"), P("y", None, None))
    return jax.shard_map(
        functools.partial(body, sizes), mesh=fine, in_specs=in_specs, out_specs=out_specs, check_vma=False
    )
```

```python
import functools
import math

import jax
import jax.numpy as jnp
from jax import lax
from jax.experimental import pallas as pl
from jax.experimental.pallas import tpu as pltpu
from jax.sharding import Mesh
from jax.sharding import PartitionSpec as P

F32, BF16, I32 = jnp.float32, jnp.bfloat16, jnp.int32
NN = (((1,), (0,)), ((), ()))
NT = (((1,), (1,)), ((), ()))
TN = (((0,), (0,)), ((), ()))
MESH = pl.DeviceIdType.MESH

TOK, CH, SUB, STEP = 256, 512, 8, 32
BS, NB = 64, 8
DP = ("zh", "core")
CTX = ("x", "zl")


def iota(shape, axis):
    return lax.broadcasted_iota(I32, shape, axis)


def dot(a, b, dims):
    return lax.dot_general(a, b, dims, preferred_element_type=F32)


def fdot(a, b, dims):
    return lax.dot_general(a, b, dims, precision=lax.Precision.HIGHEST, preferred_element_type=F32)


def split(a):
    hi = a.astype(BF16)
    return hi, (a - hi.astype(F32)).astype(BF16)


def cmul(a, b):
    return a[0] * b[0] - a[1] * b[1], a[0] * b[1] + a[1] * b[0]


def cadd(a, b):
    return a[0] + b[0], a[1] + b[1]


def cwhere(m, a, b):
    return jnp.where(m, a[0], b[0]), jnp.where(m, a[1], b[1])


def compact(full):
    lane_block = (iota((BS, 256), 1) % 128) // 32
    out = jnp.zeros((BS, 256), F32)
    for bb in range(4):
        out = jnp.where(lane_block == bb, full[BS * bb : BS * bb + BS], out)
    return out


def kernel(
    sizes, og, ps, bd_in, ac_in, rc_in, rf_in, gi, gt,
    bd, ac, rc, rf, g, pv, whi, wlo, kl, wq, un, cn, qc, rq, gc, gr, bz, bx, gsum, rcore, rx, eq, req, rz,
    lsem, ysend, yrecv, qss, qsr, bzs, bzr, bxs, bxr, css, csr, xss, xsr, zss, zsr, xas, xar,
):
    n_zh, n_core, n_x, n_zl, n_y = sizes
    n_z = n_zh * n_zl
    zh, core, x, zl, y = (lax.axis_index(a) for a in ("zh", "core", "x", "zl", "y"))
    z = zh * n_zl + zl
    rows = TOK // n_y

    def at_y(d):
        return {"y": lax.rem(y + d, n_y)}

    def at_x(d):
        return {"x": lax.rem(x + d, n_x)}

    def at_z(d):
        k = lax.rem(z + d, n_z)
        return {"zh": k // n_zl, "zl": lax.rem(k, n_zl)}

    def at_zl(d):
        return {"zl": lax.rem(zl + d, n_zl)}

    sibling = {"core": 1 - core}
    partners = (
        [at_y(d) for d in range(1, n_y)]
        + [at_x(d) for d in range(1, n_x)]
        + [at_z(d) for d in range(1, n_z)]
        + [sibling]
    )
    barrier = pltpu.get_barrier_semaphore()
    for partner in partners:
        pl.semaphore_signal(barrier, inc=1, device_id=partner, device_id_type=MESH)

    def remote(src, dst, send, recv, where):
        return pltpu.make_async_remote_copy(
            src_ref=src, dst_ref=dst, send_sem=send, recv_sem=recv, device_id=where, device_id_type=MESH
        )

    small = [
        pltpu.make_async_copy(src, dst, lsem.at[2 + i])
        for i, (src, dst) in enumerate(((ac_in, ac), (rc_in, rc), (bd_in, bd), (rf_in, rf)))
    ]
    for copy in small:
        copy.start()
    load_prev = pltpu.make_async_copy(ps.at[0], pv, lsem.at[0])
    load_prev.start()
    own_rows = pl.ds(pl.multiple_of(y * rows, rows), rows)
    load_own = pltpu.make_async_copy(
        og.at[0, :, pl.ds(pl.multiple_of(y * CH, CH), CH)], g.at[own_rows], lsem.at[1]
    )
    load_own.start()
    pl.semaphore_wait(barrier, len(partners))

    a2a = []
    for d in range(1, n_y):
        k = lax.rem(y + d, n_y)
        a2a.append(
            remote(
                og.at[0, :, pl.ds(pl.multiple_of(k * CH, CH), CH)],
                g.at[own_rows], ysend.at[d], yrecv.at[d], {"y": k},
            )
        )
        a2a[-1].start()

    for copy in small:
        copy.wait()
    pick = (iota((32, 128), 1) % 32 == iota((32, 128), 0)).astype(F32)
    acode = fdot(ac[...].astype(F32), pick, NN)
    rcode = fdot(rc[...].astype(F32), pick, NN)
    radius = 1.0 - jnp.exp2(-(4.0 + rcode * (10.0 / 1024.0)))
    angle = acode * (math.pi / 4096.0)
    lam_r, lam_i = radius * jnp.cos(angle), -radius * jnp.sin(angle)
    lam = []
    for h in range(2):
        mine = iota((NB, 128), 0) == 4 * h + iota((NB, 128), 1) // 32
        lam.append(
            tuple(
                jnp.broadcast_to(jnp.sum(jnp.where(mine, v, 0.0), axis=0, keepdims=True), (SUB, 128))
                for v in (lam_r, lam_i)
            )
        )

    r_id, t_id = iota((TOK, TOK), 0), iota((TOK, TOK), 1)
    chosen = t_id == (r_id % SUB) * STEP + r_id // SUB
    marks = jnp.where(chosen & (bd[...] == 1), 1.0, 0.0).astype(BF16)
    keep = jnp.where(dot(marks, jnp.ones((TOK, 128), BF16), NN) > 0.5, F32(0.6), F32(1.0))
    for h in range(2):
        for part in range(2):
            kl[2 * h + part] = keep * lam[h][part][0:1]

    lane = iota((BS, 256), 1)
    spread = (iota((NB, 256), 1) // 32 == iota((NB, 256), 0)).astype(F32)
    xs = [(iota((BS, 256), 0) == 2 * (lane % 32) + part).astype(F32) for part in range(2)]
    for k in (3, 2, 1, 0):
        v = fdot(rf[:, k, :], spread, TN)
        scale = 2.0 / jnp.sum(v * v, axis=0, keepdims=True)
        xs = [m - v * (scale * jnp.sum(v * m, axis=0, keepdims=True)) for m in xs]
    lane_block = (lane % 128) // 32
    for h in range(2):
        half = jnp.concatenate([m[:, 128 * h : 128 * h + 128] for m in xs], axis=1)
        for bb in range(4):
            hi, lo = split(jnp.where(lane_block == bb, half, 0.0))
            whi[h, BS * bb : BS * bb + BS, :] = hi
            wlo[h, BS * bb : BS * bb + BS, :] = lo

    def at_q(ref, q):
        return [(ref[2 * h, pl.ds(q * SUB, SUB), :], ref[2 * h + 1, pl.ds(q * SUB, SUB), :]) for h in range(2)]

    def at_t(ref, q):
        return [
            (ref[2 * h, pl.ds(q, SUB, stride=STEP), :], ref[2 * h + 1, pl.ds(q, SUB, stride=STEP), :])
            for h in range(2)
        ]

    def put_t(ref, q, value):
        for h in range(2):
            for part in range(2):
                ref[2 * h + part, pl.ds(q, SUB, stride=STEP), :] = value[h][part]

    def weights(i, w):
        for u in range(4):
            q = STEP - 1 - (4 * i + u)
            w = [cmul(a, b) for a, b in zip(at_q(kl, q), w)]
            for h in range(2):
                for part in range(2):
                    wq[2 * h + part, pl.ds(q * SUB, SUB), :] = w[h][part]
        return w

    one = (jnp.ones((SUB, 128), F32), jnp.zeros((SUB, 128), F32))
    m1 = lax.fori_loop(0, STEP // 4, weights, [one, one])
    sub = iota((SUB, 128), 0)

    def later(v, m):
        return tuple(pltpu.roll(p, SUB - m, 0) for p in v)

    zero = (jnp.zeros((SUB, 128), F32), jnp.zeros((SUB, 128), F32))
    hops, base = [], []
    for h in range(2):
        steps = [cwhere(sub < SUB - 1, m1[h], zero)]
        b = cwhere(sub < SUB - 1, later(m1[h], 1), one)
        for m in (1, 2, 4):
            if m > 1:
                steps.append(cmul(steps[-1], later(steps[-1], m // 2)))
            b = cmul(b, cwhere(sub < SUB - m, later(b, m), one))
        hops.append(steps)
        base.append(b)

    def enter(i, _):
        for u in range(4):
            q = 4 * i + u
            put_t(un, q, [cmul(a, b) for a, b in zip(at_q(wq, q), base)])
        return 0

    lax.fori_loop(0, STEP // 4, enter, 0)
    mu = [(un[2 * h, 0:1, :], un[2 * h + 1, 0:1, :]) for h in range(2)]

    def with_prev(ref, h):
        prev = pv[:, 256 * h : 256 * h + 256]
        hi, lo = split(jnp.concatenate([ref[2 * h], ref[2 * h + 1]], axis=1))
        return compact(dot(prev, hi, TN) + dot(prev, lo, TN))

    def half(k):
        return pl.ds(pl.multiple_of(k * 256, 256), 256)

    def slab(k):
        return pl.ds(pl.multiple_of(k * (BS // n_x), BS // n_x), BS // n_x)

    def scatter_x(src, dst, send, recv):
        copies = []
        for d in range(1, n_x):
            k = lax.rem(x + d, n_x)
            copies.append(remote(src.at[slab(k)], dst.at[x], send.at[d], recv.at[d], {"x": k}))
            copies[-1].start()
        dst[x] = src[slab(x), :]
        return copies

    load_prev.wait()
    for h in range(2):
        qc[:, 256 * h : 256 * h + 256] = with_prev(un, h)
    to_q = scatter_x(qc, rq, qss, qsr)

    load_own.wait()
    for copy in a2a:
        copy.wait_recv()
    for h in range(2):
        rows_h = g[:, 256 * h : 256 * h + 256]
        turned = dot(rows_h, whi[h], NN) + dot(rows_h, wlo[h], NN)
        cn[2 * h] = turned[:, :128]
        cn[2 * h + 1] = turned[:, 128:]

    def back(i, c):
        for u in range(4):
            q = STEP - 1 - (4 * i + u)
            c = [cadd(a, cmul(b, v)) for a, b, v in zip(at_t(cn, q), at_q(kl, q), c)]
            put_t(cn, q, c)
        return c

    first = lax.fori_loop(0, STEP // 4, back, [zero, zero])
    entering = []
    for h in range(2):
        v = first[h]
        for m, step in zip((1, 2, 4), hops[h]):
            v = cadd(v, cmul(step, later(v, m)))
        entering.append(cwhere(sub < SUB - 1, later(v, 1), zero))
        for part in range(2):
            bz[zl, 2 * part + h : 2 * part + h + 1, :] = v[part][0:1]
            bz[zl, 4 + 2 * part + h : 5 + 2 * part + h, :] = mu[h][part]

    zcopies = [remote(bz.at[zl], bz.at[zl], bzs.at[d], bzr.at[d], at_zl(d)) for d in range(1, n_zl)]
    for copy in zcopies:
        copy.start()

    def fix(i, _):
        for u in range(4):
            q = 4 * i + u
            put_t(cn, q, [cadd(a, cmul(b, v)) for a, b, v in zip(at_t(cn, q), at_q(wq, q), entering)])
        return 0

    lax.fori_loop(0, STEP // 4, fix, 0)
    for h in range(2):
        gc[:, 256 * h : 256 * h + 256] = with_prev(cn, h)
    to_core = remote(gc.at[:, half(1 - core)], rcore, css.at[0], csr.at[0], sibling)
    to_core.start()
    for copy in zcopies:
        copy.wait_recv()

    def pair(ref, j, at):
        return ref[j, at : at + 2, :], ref[j, at + 2 : at + 4, :]

    zero2 = (jnp.zeros((2, 128), F32), jnp.zeros((2, 128), F32))
    one2 = (jnp.ones((2, 128), F32), jnp.zeros((2, 128), F32))
    inside, passing, total, span = zero2, one2, zero2, one2
    for j in reversed(range(n_zl)):
        inside, passing = cwhere(j == zl, total, inside), cwhere(j == zl, span, passing)
        f, m = pair(bz, j, 0), pair(bz, j, 4)
        total, span = cadd(f, cmul(m, total)), cmul(m, span)
    for i, value in enumerate((total, span, inside, passing)):
        for part in range(2):
            bx[x, 4 * i + 2 * part : 4 * i + 2 * part + 2, :] = value[part]
    xcopies = [remote(bx.at[x], bx.at[x], bxs.at[d], bxr.at[d], at_x(d)) for d in range(1, n_x)]
    for copy in xcopies:
        copy.start()
    to_core.wait_recv()
    gsum[...] = gc[:, half(core)] + rcore[...]
    to_x = scatter_x(gsum, rx, xss, xsr)
    for copy in to_q:
        copy.wait_recv()
    for copy in xcopies:
        copy.wait_recv()

    beyond, entry = zero2, zero2
    sums = [zero, zero]
    for j in reversed(range(n_x)):
        here = cadd(pair(bx, j, 8), cmul(pair(bx, j, 12), beyond))
        entry = cwhere(j == x, here, entry)
        beyond = cadd(pair(bx, j, 0), cmul(pair(bx, j, 4), beyond))
        for h in range(2):
            e = (here[0][h : h + 1], here[1][h : h + 1])
            weight = (rq[j, :, 256 * h : 256 * h + 128], rq[j, :, 256 * h + 128 : 256 * h + 256])
            term = cmul(e, weight)
            sums[h] = term if j == n_x - 1 else cadd(sums[h], term)
    for h in range(2):
        for part in range(2):
            at = 256 * h + 128 * part
            eq[:, at : at + 128] = sums[h][part]
    to_core_2 = remote(eq.at[:, half(1 - core)], req, css.at[1], csr.at[1], sibling)
    to_core_2.start()
    for copy in to_x:
        copy.wait_recv()
    owned = jnp.sum(rx[...], axis=0) + eq[:, half(core)]
    to_core_2.wait_recv()
    rz[z] = owned + req[...]
    to_z = [remote(rz.at[z], rz.at[z], zss.at[d], zsr.at[d], at_z(d)) for d in range(1, n_z)]
    for copy in to_z:
        copy.start()
    for h in range(2):
        e = (entry[0][h : h + 1], entry[1][h : h + 1])
        c = cadd((cn[2 * h], cn[2 * h + 1]), cmul(e, (un[2 * h], un[2 * h + 1])))
        hi, lo = split(jnp.concatenate(c, axis=1))
        adj = dot(hi, whi[h], NT) + dot(lo, whi[h], NT) + dot(hi, wlo[h], NT)
        gi[0, :, 256 * h : 256 * h + 256] = adj.astype(BF16)
    for copy in to_z:
        copy.wait_recv()
    gr[slab(x), half(core)] = jnp.sum(rz[...], axis=0)
    mine = gr.at[slab(x), half(core)]
    back_x = [remote(mine, mine, xas.at[d], xar.at[d], at_x(d)) for d in range(1, n_x)]
    for copy in back_x:
        copy.start()
    for copy in back_x:
        copy.wait_recv()
    ours = gr.at[:, half(core)]
    back_core = remote(ours, ours, css.at[2], csr.at[2], sibling)
    back_core.start()

    def finish(h):
        hi, lo = split(gr[:, half(h)])
        out = dot(whi[h], hi, NT) + dot(whi[h], lo, NT) + dot(wlo[h], hi, NT)
        gt[pl.ds(4 * h, 4)] = out.reshape(4, BS, BS)

    finish(core)
    back_core.wait_recv()
    finish(1 - core)

    for copy in a2a + to_q + zcopies + [to_core] + xcopies + to_x + [to_core_2] + to_z + back_x + [back_core]:
        copy.wait_send()


def body(sizes, *operands):
    n_zh, n_core, n_x, n_zl, n_y = sizes
    n_z = n_zh * n_zl
    slab = BS // n_x
    vmem, anywhere = pl.BlockSpec(memory_space=pltpu.VMEM), pl.BlockSpec(memory_space=pltpu.HBM)
    plane = pltpu.VMEM((4, TOK, 128), F32)
    dma = pltpu.SemaphoreType.DMA
    return pl.pallas_call(
        functools.partial(kernel, sizes),
        out_shape=(
            jax.ShapeDtypeStruct((1, TOK, CH), BF16),
            jax.ShapeDtypeStruct((NB, BS, BS), F32),
        ),
        in_specs=[anywhere] * 6,
        out_specs=(vmem, vmem),
        scratch_shapes=[
            pltpu.VMEM((1, TOK), I32),
            pltpu.VMEM((NB, 32), I32),
            pltpu.VMEM((NB, 32), I32),
            pltpu.VMEM((NB, 4, BS), F32),
            pltpu.VMEM((TOK, CH), BF16),
            pltpu.VMEM((TOK, CH), BF16),
            pltpu.VMEM((2, 256, 256), BF16),
            pltpu.VMEM((2, 256, 256), BF16),
            plane, plane, plane, plane,
            pltpu.VMEM((BS, CH), F32),
            pltpu.VMEM((n_x, slab, CH), F32),
            pltpu.VMEM((BS, CH), F32),
            pltpu.VMEM((BS, CH), F32),
            pltpu.VMEM((n_zl, 8, 128), F32),
            pltpu.VMEM((n_x, 16, 128), F32),
            pltpu.VMEM((BS, 256), F32),
            pltpu.VMEM((BS, 256), F32),
            pltpu.VMEM((n_x, slab, 256), F32),
            pltpu.VMEM((slab, CH), F32),
            pltpu.VMEM((slab, 256), F32),
            pltpu.VMEM((n_z, slab, 256), F32),
            dma((6,)),
            dma((n_y,)), dma((n_y,)),
            dma((n_x,)), dma((n_x,)),
            dma((n_zl,)), dma((n_zl,)),
            dma((n_x,)), dma((n_x,)),
            dma((3,)), dma((3,)),
            dma((n_x,)), dma((n_x,)),
            dma((n_z,)), dma((n_z,)),
            dma((n_x,)), dma((n_x,)),
        ],
        compiler_params=pltpu.CompilerParams(
            collective_id=0, has_side_effects=True, vmem_limit_bytes=32 * 2**20
        ),
    )(*(pltpu.with_memory_space_constraint(a, pltpu.HBM) for a in operands))


def solution(mesh):
    n_dp, n_ctx, n_y = (mesh.shape[a] for a in ("dp", "ctx", "tensor"))
    n_x = min(8, n_ctx // 2)
    sizes = (n_dp // 2, 2, n_x, n_ctx // n_x, n_y)
    fine = Mesh(mesh.devices.reshape(sizes), ("zh", "core", "x", "zl", "y"))
    in_specs = (
        P(DP, (*CTX, "y"), None),
        P(DP, CTX, "y"),
        P(DP, CTX),
        P("y", None),
        P("y", None),
        P("y", None, None),
    )
    out_specs = (P(DP, CTX, "y"), P("y", None, None))
    return jax.shard_map(
        functools.partial(body, sizes), mesh=fine, in_specs=in_specs, out_specs=out_specs, check_vma=False
    )
```

```python
import functools
import math

import jax
import jax.numpy as jnp
from jax import lax
from jax.experimental import pallas as pl
from jax.experimental.pallas import tpu as pltpu
from jax.sharding import Mesh
from jax.sharding import PartitionSpec as P

F32, BF16, I32 = jnp.float32, jnp.bfloat16, jnp.int32
NN = (((1,), (0,)), ((), ()))
NT = (((1,), (1,)), ((), ()))
TN = (((0,), (0,)), ((), ()))
MESH = pl.DeviceIdType.MESH

TOK, CH, SUB, STEP = 256, 512, 8, 32
BS, NB = 64, 8
DP = ("zh", "core")
CTX = ("x", "zl")


def iota(shape, axis):
    return lax.broadcasted_iota(I32, shape, axis)


def dot(a, b, dims):
    return lax.dot_general(a, b, dims, preferred_element_type=F32)


def fdot(a, b, dims):
    return lax.dot_general(a, b, dims, precision=lax.Precision.HIGHEST, preferred_element_type=F32)


def split(a):
    hi = a.astype(BF16)
    return hi, (a - hi.astype(F32)).astype(BF16)


def cmul(a, b):
    return a[0] * b[0] - a[1] * b[1], a[0] * b[1] + a[1] * b[0]


def cadd(a, b):
    return a[0] + b[0], a[1] + b[1]


def cwhere(m, a, b):
    return jnp.where(m, a[0], b[0]), jnp.where(m, a[1], b[1])


def far_first(count):
    return sorted(range(1, count), key=lambda d: -min(d, count - d))


def compact(full):
    lane_block = (iota((BS, 256), 1) % 128) // 32
    out = jnp.zeros((BS, 256), F32)
    for bb in range(4):
        out = jnp.where(lane_block == bb, full[BS * bb : BS * bb + BS], out)
    return out


def kernel(
    sizes, og, ps, bd_in, ac_in, rc_in, rf_in, gi, gt,
    bd, ac, rc, rf, g, pv, whi, wlo, kl, wq, un, cn, qc, rq, gc, gr, bc, gsum, rcore, rx, eq, req, rz,
    lsem, ysend, yrecv, qss, qsr, bcs, bcr, css, csr, xss, xsr, zss, zsr, xas, xar, ready,
):
    n_zh, n_core, n_x, n_zl, n_y = sizes
    n_z = n_zh * n_zl
    zh, core, x, zl, y = (lax.axis_index(a) for a in ("zh", "core", "x", "zl", "y"))
    z = zh * n_zl + zl
    rows = TOK // n_y

    def at_y(d):
        return {"y": lax.rem(y + d, n_y)}

    def at_x(d):
        return {"x": lax.rem(x + d, n_x)}

    def at_z(d):
        k = lax.rem(z + d, n_z)
        return {"zh": k // n_zl, "zl": lax.rem(k, n_zl)}

    def at_ctx(d, e):
        return {"x": lax.rem(x + d, n_x), "zl": lax.rem(zl + e, n_zl)}

    sibling = {"core": 1 - core}
    partners = (
        [at_y(d) for d in range(1, n_y)]
        + [at_x(d) for d in range(1, n_x)]
        + [at_z(d) for d in range(1, n_z)]
        + [sibling]
    )
    barrier = pltpu.get_barrier_semaphore()
    for partner in partners:
        pl.semaphore_signal(barrier, inc=1, device_id=partner, device_id_type=MESH)

    def remote(src, dst, send, recv, where):
        return pltpu.make_async_remote_copy(
            src_ref=src, dst_ref=dst, send_sem=send, recv_sem=recv, device_id=where, device_id_type=MESH
        )

    small = [
        pltpu.make_async_copy(src, dst, lsem.at[2 + i])
        for i, (src, dst) in enumerate(((ac_in, ac), (rc_in, rc), (bd_in, bd), (rf_in, rf)))
    ]
    for copy in small:
        copy.start()
    load_prev = pltpu.make_async_copy(ps.at[0], pv, lsem.at[0])
    load_prev.start()
    own_rows = pl.ds(pl.multiple_of(y * rows, rows), rows)
    load_own = pltpu.make_async_copy(
        og.at[0, :, pl.ds(pl.multiple_of(y * CH, CH), CH)], g.at[own_rows], lsem.at[1]
    )
    load_own.start()
    pl.semaphore_wait(barrier, len(partners))
    for d in range(1, n_x):
        pl.semaphore_signal(ready, inc=1, device_id=at_x(d), device_id_type=MESH)

    a2a = []
    for d in range(1, n_y):
        k = lax.rem(y + d, n_y)
        a2a.append(
            remote(
                og.at[0, :, pl.ds(pl.multiple_of(k * CH, CH), CH)],
                g.at[own_rows], ysend.at[d], yrecv.at[d], {"y": k},
            )
        )
        a2a[-1].start()

    for copy in small:
        copy.wait()
    pick = (iota((32, 128), 1) % 32 == iota((32, 128), 0)).astype(F32)
    acode = fdot(ac[...].astype(F32), pick, NN)
    rcode = fdot(rc[...].astype(F32), pick, NN)
    radius = 1.0 - jnp.exp2(-(4.0 + rcode * (10.0 / 1024.0)))
    angle = acode * (math.pi / 4096.0)
    lam_r, lam_i = radius * jnp.cos(angle), -radius * jnp.sin(angle)
    lam = []
    for h in range(2):
        mine = iota((NB, 128), 0) == 4 * h + iota((NB, 128), 1) // 32
        lam.append(
            tuple(
                jnp.broadcast_to(jnp.sum(jnp.where(mine, v, 0.0), axis=0, keepdims=True), (SUB, 128))
                for v in (lam_r, lam_i)
            )
        )

    r_id, t_id = iota((TOK, TOK), 0), iota((TOK, TOK), 1)
    chosen = t_id == (r_id % SUB) * STEP + r_id // SUB
    marks = jnp.where(chosen & (bd[...] == 1), 1.0, 0.0).astype(BF16)
    keep = jnp.where(dot(marks, jnp.ones((TOK, 128), BF16), NN) > 0.5, F32(0.6), F32(1.0))
    for h in range(2):
        for part in range(2):
            kl[2 * h + part] = keep * lam[h][part][0:1]

    lane = iota((BS, 256), 1)
    spread = (iota((NB, 256), 1) // 32 == iota((NB, 256), 0)).astype(F32)
    xs = [(iota((BS, 256), 0) == 2 * (lane % 32) + part).astype(F32) for part in range(2)]
    for k in (3, 2, 1, 0):
        v = fdot(rf[:, k, :], spread, TN)
        scale = 2.0 / jnp.sum(v * v, axis=0, keepdims=True)
        xs = [m - v * (scale * jnp.sum(v * m, axis=0, keepdims=True)) for m in xs]
    lane_block = (lane % 128) // 32
    for h in range(2):
        half = jnp.concatenate([m[:, 128 * h : 128 * h + 128] for m in xs], axis=1)
        for bb in range(4):
            hi, lo = split(jnp.where(lane_block == bb, half, 0.0))
            whi[h, BS * bb : BS * bb + BS, :] = hi
            wlo[h, BS * bb : BS * bb + BS, :] = lo

    def at_q(ref, q):
        return [(ref[2 * h, pl.ds(q * SUB, SUB), :], ref[2 * h + 1, pl.ds(q * SUB, SUB), :]) for h in range(2)]

    def at_t(ref, q):
        return [
            (ref[2 * h, pl.ds(q, SUB, stride=STEP), :], ref[2 * h + 1, pl.ds(q, SUB, stride=STEP), :])
            for h in range(2)
        ]

    def put_t(ref, q, value):
        for h in range(2):
            for part in range(2):
                ref[2 * h + part, pl.ds(q, SUB, stride=STEP), :] = value[h][part]

    def weights(i, w):
        for u in range(4):
            q = STEP - 1 - (4 * i + u)
            w = [cmul(a, b) for a, b in zip(at_q(kl, q), w)]
            for h in range(2):
                for part in range(2):
                    wq[2 * h + part, pl.ds(q * SUB, SUB), :] = w[h][part]
        return w

    one = (jnp.ones((SUB, 128), F32), jnp.zeros((SUB, 128), F32))
    m1 = lax.fori_loop(0, STEP // 4, weights, [one, one])
    sub = iota((SUB, 128), 0)

    def later(v, m):
        return tuple(pltpu.roll(p, SUB - m, 0) for p in v)

    zero = (jnp.zeros((SUB, 128), F32), jnp.zeros((SUB, 128), F32))
    hops, base = [], []
    for h in range(2):
        steps = [cwhere(sub < SUB - 1, m1[h], zero)]
        b = cwhere(sub < SUB - 1, later(m1[h], 1), one)
        for m in (1, 2, 4):
            if m > 1:
                steps.append(cmul(steps[-1], later(steps[-1], m // 2)))
            b = cmul(b, cwhere(sub < SUB - m, later(b, m), one))
        hops.append(steps)
        base.append(b)

    def enter(i, _):
        for u in range(4):
            q = 4 * i + u
            put_t(un, q, [cmul(a, b) for a, b in zip(at_q(wq, q), base)])
        return 0

    lax.fori_loop(0, STEP // 4, enter, 0)
    mu = [(un[2 * h, 0:1, :], un[2 * h + 1, 0:1, :]) for h in range(2)]

    def with_prev(ref, h):
        prev = pv[:, 256 * h : 256 * h + 256]
        hi, lo = split(jnp.concatenate([ref[2 * h], ref[2 * h + 1]], axis=1))
        return compact(dot(prev, hi, TN) + dot(prev, lo, TN))

    def half(k):
        return pl.ds(pl.multiple_of(k * 256, 256), 256)

    n_own = n_x // 2
    deep = BS // n_own

    def slab(k):
        return pl.ds(pl.multiple_of(lax.rem(k, n_own) * deep, deep), deep)

    def scatter_x(src, dst, send, recv):
        copies = []
        for d in far_first(n_x):
            k = lax.rem(x + d, n_x)
            copies.append(remote(src.at[slab(k)], dst.at[x], send.at[d], recv.at[d], {"x": k}))
            copies[-1].start()
        dst[x] = src[slab(x), :]
        return copies

    load_prev.wait()
    for h in range(2):
        qc[:, 256 * h : 256 * h + 256] = with_prev(un, h)
    to_q = scatter_x(qc, rq, qss, qsr)

    load_own.wait()
    for copy in a2a:
        copy.wait_recv()
    for h in range(2):
        rows_h = g[:, 256 * h : 256 * h + 256]
        turned = dot(rows_h, whi[h], NN) + dot(rows_h, wlo[h], NN)
        cn[2 * h] = turned[:, :128]
        cn[2 * h + 1] = turned[:, 128:]

    def back(i, c):
        for u in range(4):
            q = STEP - 1 - (4 * i + u)
            c = [cadd(a, cmul(b, v)) for a, b, v in zip(at_t(cn, q), at_q(kl, q), c)]
            put_t(cn, q, c)
        return c

    first = lax.fori_loop(0, STEP // 4, back, [zero, zero])
    entering, me = [], x * n_zl + zl
    for h in range(2):
        v = first[h]
        for m, step in zip((1, 2, 4), hops[h]):
            v = cadd(v, cmul(step, later(v, m)))
        entering.append(cwhere(sub < SUB - 1, later(v, 1), zero))
        for part in range(2):
            bc[me, 2 * part + h : 2 * part + h + 1, :] = v[part][0:1]
            bc[me, 4 + 2 * part + h : 5 + 2 * part + h, :] = mu[h][part]

    pl.semaphore_wait(ready, n_x - 1)
    offsets = [(d, e) for d in range(n_x) for e in range(n_zl) if d or e]
    offsets.sort(key=lambda o: -min(o[0], n_x - o[0]) - min(o[1], n_zl - o[1]))
    carries = [
        remote(bc.at[me], bc.at[me], bcs.at[i], bcr.at[i], at_ctx(*o)) for i, o in enumerate(offsets)
    ]
    for copy in carries:
        copy.start()

    def fix(i, _):
        for u in range(4):
            q = 4 * i + u
            put_t(cn, q, [cadd(a, cmul(b, v)) for a, b, v in zip(at_t(cn, q), at_q(wq, q), entering)])
        return 0

    lax.fori_loop(0, STEP // 4, fix, 0)
    for h in range(2):
        gc[:, 256 * h : 256 * h + 256] = with_prev(cn, h)
    to_core = remote(gc.at[:, half(1 - core)], rcore, css.at[0], csr.at[0], sibling)
    to_core.start()
    to_core.wait_recv()
    gsum[...] = gc[:, half(core)] + rcore[...]
    to_x = scatter_x(gsum, rx, xss, xsr)
    for copy in to_q:
        copy.wait_recv()
    for copy in carries:
        copy.wait_recv()

    def pair(j, at):
        return bc[j, at : at + 2, :], bc[j, at + 2 : at + 4, :]

    zero2 = (jnp.zeros((2, 128), F32), jnp.zeros((2, 128), F32))
    one2 = (jnp.ones((2, 128), F32), jnp.zeros((2, 128), F32))
    chains = []
    for k in range(n_x):
        inside, passing, total, span = zero2, one2, zero2, one2
        for j in reversed(range(n_zl)):
            inside, passing = cwhere(j == zl, total, inside), cwhere(j == zl, span, passing)
            f, m = pair(k * n_zl + j, 0), pair(k * n_zl + j, 4)
            total, span = cadd(f, cmul(m, total)), cmul(m, span)
        chains.append((inside, passing, total, span))
    beyond, entry = zero2, zero2
    sums = [zero, zero]
    for j in reversed(range(n_x)):
        inside, passing, total, span = chains[j]
        here = cadd(inside, cmul(passing, beyond))
        entry = cwhere(j == x, here, entry)
        beyond = cadd(total, cmul(span, beyond))
        for h in range(2):
            e = (here[0][h : h + 1], here[1][h : h + 1])
            weight = (rq[j, :, 256 * h : 256 * h + 128], rq[j, :, 256 * h + 128 : 256 * h + 256])
            term = cmul(e, weight)
            sums[h] = term if j == n_x - 1 else cadd(sums[h], term)
    for h in range(2):
        for part in range(2):
            at = 256 * h + 128 * part
            eq[:, at : at + 128] = sums[h][part]
    to_core_2 = remote(eq.at[:, half(1 - core)], req, css.at[1], csr.at[1], sibling)
    to_core_2.start()
    for copy in to_x:
        copy.wait_recv()
    owned = jnp.sum(rx[...], axis=0) + eq[:, half(core)]
    to_core_2.wait_recv()
    rz[z] = owned + req[...]
    to_z = [remote(rz.at[z], rz.at[z], zss.at[d], zsr.at[d], at_z(d)) for d in far_first(n_z)]
    for copy in to_z:
        copy.start()
    for h in range(2):
        e = (entry[0][h : h + 1], entry[1][h : h + 1])
        c = cadd((cn[2 * h], cn[2 * h + 1]), cmul(e, (un[2 * h], un[2 * h + 1])))
        hi, lo = split(jnp.concatenate(c, axis=1))
        adj = dot(hi, whi[h], NT) + dot(lo, whi[h], NT) + dot(hi, wlo[h], NT)
        gi[0, :, 256 * h : 256 * h + 256] = adj.astype(BF16)
    for copy in to_z:
        copy.wait_recv()
    hi, lo = split(jnp.sum(rz[...], axis=0))
    gr[slab(x), half(core)] = dot(hi, whi[core], NT) + dot(lo, whi[core], NT) + dot(hi, wlo[core], NT)
    mine = gr.at[slab(x), half(core)]
    back_x = []
    for i, d in enumerate(far_first(n_own)):
        where = at_x(d if d <= n_own // 2 else n_x - n_own + d)
        back_x.append(remote(mine, mine, xas.at[i], xar.at[i], where))
        back_x[-1].start()
    for copy in back_x:
        copy.wait_recv()
    ours = gr.at[:, half(core)]
    back_core = remote(ours, ours, css.at[2], csr.at[2], sibling)
    back_core.start()

    def finish(h):
        gt[pl.ds(4 * h, 4)] = gr[:, half(h)].T.reshape(4, BS, BS)

    finish(core)
    back_core.wait_recv()
    finish(1 - core)

    for copy in a2a + to_q + carries + [to_core] + to_x + [to_core_2] + to_z + back_x + [back_core]:
        copy.wait_send()


def body(sizes, *operands):
    n_zh, n_core, n_x, n_zl, n_y = sizes
    n_z = n_zh * n_zl
    slab = BS // (n_x // 2)
    vmem, anywhere = pl.BlockSpec(memory_space=pltpu.VMEM), pl.BlockSpec(memory_space=pltpu.HBM)
    plane = pltpu.VMEM((4, TOK, 128), F32)
    dma = pltpu.SemaphoreType.DMA
    return pl.pallas_call(
        functools.partial(kernel, sizes),
        out_shape=(
            jax.ShapeDtypeStruct((1, TOK, CH), BF16),
            jax.ShapeDtypeStruct((NB, BS, BS), F32),
        ),
        in_specs=[anywhere] * 6,
        out_specs=(vmem, vmem),
        scratch_shapes=[
            pltpu.VMEM((1, TOK), I32),
            pltpu.VMEM((NB, 32), I32),
            pltpu.VMEM((NB, 32), I32),
            pltpu.VMEM((NB, 4, BS), F32),
            pltpu.VMEM((TOK, CH), BF16),
            pltpu.VMEM((TOK, CH), BF16),
            pltpu.VMEM((2, 256, 256), BF16),
            pltpu.VMEM((2, 256, 256), BF16),
            plane, plane, plane, plane,
            pltpu.VMEM((BS, CH), F32),
            pltpu.VMEM((n_x, slab, CH), F32),
            pltpu.VMEM((BS, CH), F32),
            pltpu.VMEM((BS, CH), F32),
            pltpu.VMEM((n_x * n_zl, 8, 128), F32),
            pltpu.VMEM((BS, 256), F32),
            pltpu.VMEM((BS, 256), F32),
            pltpu.VMEM((n_x, slab, 256), F32),
            pltpu.VMEM((slab, CH), F32),
            pltpu.VMEM((slab, 256), F32),
            pltpu.VMEM((n_z, slab, 256), F32),
            dma((6,)),
            dma((n_y,)), dma((n_y,)),
            dma((n_x,)), dma((n_x,)),
            dma((n_x * n_zl,)), dma((n_x * n_zl,)),
            dma((3,)), dma((3,)),
            dma((n_x,)), dma((n_x,)),
            dma((n_z,)), dma((n_z,)),
            dma((n_x,)), dma((n_x,)),
            pltpu.SemaphoreType.REGULAR,
        ],
        compiler_params=pltpu.CompilerParams(
            collective_id=0, has_side_effects=True, vmem_limit_bytes=32 * 2**20
        ),
    )(*(pltpu.with_memory_space_constraint(a, pltpu.HBM) for a in operands))


def solution(mesh):
    n_dp, n_ctx, n_y = (mesh.shape[a] for a in ("dp", "ctx", "tensor"))
    n_x = min(8, n_ctx // 2)
    sizes = (n_dp // 2, 2, n_x, n_ctx // n_x, n_y)
    fine = Mesh(mesh.devices.reshape(sizes), ("zh", "core", "x", "zl", "y"))
    in_specs = (
        P(DP, (*CTX, "y"), None),
        P(DP, CTX, "y"),
        P(DP, CTX),
        P("y", None),
        P("y", None),
        P("y", None, None),
    )
    out_specs = (P(DP, CTX, "y"), P("y", None, None))
    return jax.shard_map(
        functools.partial(body, sizes), mesh=fine, in_specs=in_specs, out_specs=out_specs, check_vma=False
    )
```

```python
import functools
import math

import jax
import jax.numpy as jnp
from jax import lax
from jax.experimental import pallas as pl
from jax.experimental.pallas import tpu as pltpu
from jax.sharding import Mesh
from jax.sharding import PartitionSpec as P

F32, BF16, I32 = jnp.float32, jnp.bfloat16, jnp.int32
NN = (((1,), (0,)), ((), ()))
NT = (((1,), (1,)), ((), ()))
TN = (((0,), (0,)), ((), ()))
MESH = pl.DeviceIdType.MESH

TOK, CH, SUB, STEP = 256, 512, 8, 32
BS, NB = 64, 8
DP = ("zh", "core")
CTX = ("x", "zl")


def iota(shape, axis):
    return lax.broadcasted_iota(I32, shape, axis)


def dot(a, b, dims):
    return lax.dot_general(a, b, dims, preferred_element_type=F32)


def fdot(a, b, dims):
    return lax.dot_general(a, b, dims, precision=lax.Precision.HIGHEST, preferred_element_type=F32)


def split(a):
    hi = a.astype(BF16)
    return hi, (a - hi.astype(F32)).astype(BF16)


def cmul(a, b):
    return a[0] * b[0] - a[1] * b[1], a[0] * b[1] + a[1] * b[0]


def cadd(a, b):
    return a[0] + b[0], a[1] + b[1]


def cwhere(m, a, b):
    return jnp.where(m, a[0], b[0]), jnp.where(m, a[1], b[1])


def far_first(count):
    return sorted(range(1, count), key=lambda d: -min(d, count - d))


def compact(full):
    lane_block = (iota((BS, 256), 1) % 128) // 32
    out = jnp.zeros((BS, 256), F32)
    for bb in range(4):
        out = jnp.where(lane_block == bb, full[BS * bb : BS * bb + BS], out)
    return out


def kernel(
    sizes, og, ps, bd_in, ac_in, rc_in, rf_in, gi, gt,
    bd, ac, rc, rf, g, pv, whi, wlo, kl, wq, fw, un, cn, qc, rq, gc, gr, bc, gsum, rcore, rx, eq, req, rz,
    lsem, ysend, yrecv, qss, qsr, bcs, bcr, css, csr, xss, xsr, zss, zsr, xas, xar, ready,
):
    n_zh, n_core, n_x, n_zl, n_y = sizes
    n_z = n_zh * n_zl
    zh, core, x, zl, y = (lax.axis_index(a) for a in ("zh", "core", "x", "zl", "y"))
    z = zh * n_zl + zl
    rows = TOK // n_y

    def at_y(d):
        return {"y": lax.rem(y + d, n_y)}

    def at_x(d):
        return {"x": lax.rem(x + d, n_x)}

    def at_z(d):
        k = lax.rem(z + d, n_z)
        return {"zh": k // n_zl, "zl": lax.rem(k, n_zl)}

    def at_ctx(d, e):
        return {"x": lax.rem(x + d, n_x), "zl": lax.rem(zl + e, n_zl)}

    sibling = {"core": 1 - core}
    partners = (
        [at_y(d) for d in far_first(n_y)]
        + [at_x(d) for d in far_first(n_x)]
        + [at_z(d) for d in far_first(n_z)]
        + [sibling]
    )
    barrier = pltpu.get_barrier_semaphore()
    for partner in partners:
        pl.semaphore_signal(barrier, inc=1, device_id=partner, device_id_type=MESH)

    def remote(src, dst, send, recv, where):
        return pltpu.make_async_remote_copy(
            src_ref=src, dst_ref=dst, send_sem=send, recv_sem=recv, device_id=where, device_id_type=MESH
        )

    small = [
        pltpu.make_async_copy(src, dst, lsem.at[2 + i])
        for i, (src, dst) in enumerate(((ac_in, ac), (rc_in, rc), (bd_in, bd), (rf_in, rf)))
    ]
    for copy in small:
        copy.start()
    load_prev = pltpu.make_async_copy(ps.at[0], pv, lsem.at[0])
    load_prev.start()
    own_rows = pl.ds(pl.multiple_of(y * rows, rows), rows)
    load_own = pltpu.make_async_copy(
        og.at[0, :, pl.ds(pl.multiple_of(y * CH, CH), CH)], g.at[own_rows], lsem.at[1]
    )
    load_own.start()
    for copy in small:
        copy.wait()
    pick = (iota((32, 128), 1) % 32 == iota((32, 128), 0)).astype(F32)
    acode = fdot(ac[...].astype(F32), pick, NN)
    rcode = fdot(rc[...].astype(F32), pick, NN)
    radius = 1.0 - jnp.exp2(-(4.0 + rcode * (10.0 / 1024.0)))
    angle = acode * (math.pi / 4096.0)
    lam_r, lam_i = radius * jnp.cos(angle), -radius * jnp.sin(angle)
    lam = []
    for h in range(2):
        mine = iota((NB, 128), 0) == 4 * h + iota((NB, 128), 1) // 32
        lam.append(
            tuple(
                jnp.broadcast_to(jnp.sum(jnp.where(mine, v, 0.0), axis=0, keepdims=True), (SUB, 128))
                for v in (lam_r, lam_i)
            )
        )

    r_id, t_id = iota((TOK, TOK), 0), iota((TOK, TOK), 1)
    chosen = t_id == (r_id % SUB) * STEP + r_id // SUB
    marks = jnp.where(chosen & (bd[...] == 1), 1.0, 0.0).astype(BF16)
    keep = jnp.where(dot(marks, jnp.ones((TOK, 128), BF16), NN) > 0.5, F32(0.6), F32(1.0))
    for h in range(2):
        for part in range(2):
            kl[2 * h + part] = keep * lam[h][part][0:1]

    pl.semaphore_wait(barrier, len(partners))
    for d in range(1, n_x):
        pl.semaphore_signal(ready, inc=1, device_id=at_x(d), device_id_type=MESH)

    a2a = []
    for d in range(1, n_y):
        k = lax.rem(y + d, n_y)
        a2a.append(
            remote(
                og.at[0, :, pl.ds(pl.multiple_of(k * CH, CH), CH)],
                g.at[own_rows], ysend.at[d], yrecv.at[d], {"y": k},
            )
        )
        a2a[-1].start()

    lane = iota((BS, 256), 1)
    spread = (iota((NB, 256), 1) // 32 == iota((NB, 256), 0)).astype(F32)
    xs = [(iota((BS, 256), 0) == 2 * (lane % 32) + part).astype(F32) for part in range(2)]
    for k in (3, 2, 1, 0):
        v = fdot(rf[:, k, :], spread, TN)
        scale = 2.0 / jnp.sum(v * v, axis=0, keepdims=True)
        xs = [m - v * (scale * jnp.sum(v * m, axis=0, keepdims=True)) for m in xs]
    lane_block = (lane % 128) // 32
    for h in range(2):
        half = jnp.concatenate([m[:, 128 * h : 128 * h + 128] for m in xs], axis=1)
        for bb in range(4):
            hi, lo = split(jnp.where(lane_block == bb, half, 0.0))
            whi[h, BS * bb : BS * bb + BS, :] = hi
            wlo[h, BS * bb : BS * bb + BS, :] = lo

    def at_q(ref, q):
        return [(ref[2 * h, pl.ds(q * SUB, SUB), :], ref[2 * h + 1, pl.ds(q * SUB, SUB), :]) for h in range(2)]

    def at_t(ref, q):
        return [
            (ref[2 * h, pl.ds(q, SUB, stride=STEP), :], ref[2 * h + 1, pl.ds(q, SUB, stride=STEP), :])
            for h in range(2)
        ]

    def put_t(ref, q, value):
        for h in range(2):
            for part in range(2):
                ref[2 * h + part, pl.ds(q, SUB, stride=STEP), :] = value[h][part]

    def weights(i, w):
        for u in range(4):
            q = STEP - 1 - (4 * i + u)
            w = [cmul(a, b) for a, b in zip(at_q(kl, q), w)]
            for h in range(2):
                for part in range(2):
                    wq[2 * h + part, pl.ds(q * SUB, SUB), :] = w[h][part]
        return w

    one = (jnp.ones((SUB, 128), F32), jnp.zeros((SUB, 128), F32))
    m1 = lax.fori_loop(0, STEP // 4, weights, [one, one])
    sub = iota((SUB, 128), 0)

    def later(v, m):
        return tuple(pltpu.roll(p, SUB - m, 0) for p in v)

    def earlier(v, m):
        return tuple(pltpu.roll(p, m, 0) for p in v)

    zero = (jnp.zeros((SUB, 128), F32), jnp.zeros((SUB, 128), F32))
    hops, base, head = [], [], []
    for h in range(2):
        steps = [cwhere(sub < SUB - 1, m1[h], zero)]
        b = cwhere(sub < SUB - 1, later(m1[h], 1), one)
        for m in (1, 2, 4):
            if m > 1:
                steps.append(cmul(steps[-1], later(steps[-1], m // 2)))
            b = cmul(b, cwhere(sub < SUB - m, later(b, m), one))
        a = cwhere(sub >= 1, earlier(m1[h], 1), one)
        for m in (1, 2, 4):
            a = cmul(a, cwhere(sub >= m, earlier(a, m), one))
        hops.append(steps)
        base.append(b)
        head.append(a)

    def enter(i, _):
        for u in range(4):
            q = 4 * i + u
            put_t(un, q, [cmul(a, b) for a, b in zip(at_q(wq, q), base)])
        return 0

    lax.fori_loop(0, STEP // 4, enter, 0)

    def leave(i, w):
        for u in range(4):
            q = 4 * i + u
            put_t(fw, q, w)
            w = [cmul(a, b) for a, b in zip(at_q(kl, q), w)]
        return w

    lax.fori_loop(0, STEP // 4, leave, head)
    mu = [(un[2 * h, 0:1, :], un[2 * h + 1, 0:1, :]) for h in range(2)]

    def with_prev(ref, h):
        prev = pv[:, 256 * h : 256 * h + 256]
        hi, lo = split(jnp.concatenate([ref[2 * h], ref[2 * h + 1]], axis=1))
        return compact(dot(prev, hi, TN) + dot(prev, lo, TN))

    def half(k):
        return pl.ds(pl.multiple_of(k * 256, 256), 256)

    n_own = n_x
    deep = BS // n_own

    def slab(k):
        return pl.ds(pl.multiple_of(lax.rem(k, n_own) * deep, deep), deep)

    def scatter_x(src, dst, send, recv):
        copies = []
        for d in far_first(n_x):
            k = lax.rem(x + d, n_x)
            copies.append(remote(src.at[slab(k)], dst.at[x], send.at[d], recv.at[d], {"x": k}))
            copies[-1].start()
        dst[x] = src[slab(x), :]
        return copies

    load_prev.wait()
    for h in range(2):
        qc[:, 256 * h : 256 * h + 256] = with_prev(un, h)
    to_q = scatter_x(qc, rq, qss, qsr)

    def piece(k, total):
        at = pl.ds(pl.multiple_of(k * rows, rows), rows)
        out = []
        for h in range(2):
            part = g[at, 256 * h : 256 * h + 256]
            turned = dot(part, whi[h], NN) + dot(part, wlo[h], NN)
            c = turned[:, :128], turned[:, 128:]
            cn[2 * h, at, :], cn[2 * h + 1, at, :] = c
            term = cmul((fw[2 * h, at, :], fw[2 * h + 1, at, :]), c)
            out.append(cadd(total[h], tuple(jnp.sum(v.reshape(rows // 8, 8, 128), axis=0) for v in term)))
        return out

    load_own.wait()
    carry = piece(y, [zero, zero])
    for d in reversed(far_first(n_y)):
        a2a[d - 1].wait_recv()
        carry = piece(lax.rem(y + n_y - d, n_y), carry)
    me = x * n_zl + zl
    for h in range(2):
        for part in range(2):
            bc[me, 2 * part + h : 2 * part + h + 1, :] = jnp.sum(carry[h][part], axis=0, keepdims=True)
            bc[me, 4 + 2 * part + h : 5 + 2 * part + h, :] = mu[h][part]

    pl.semaphore_wait(ready, n_x - 1)
    offsets = [(d, e) for d in range(n_x) for e in range(n_zl) if d or e]
    offsets.sort(key=lambda o: -min(o[0], n_x - o[0]) - min(o[1], n_zl - o[1]))
    carries = [
        remote(bc.at[me], bc.at[me], bcs.at[i], bcr.at[i], at_ctx(*o)) for i, o in enumerate(offsets)
    ]
    for copy in carries:
        copy.start()

    def back(i, c):
        for u in range(4):
            q = STEP - 1 - (4 * i + u)
            c = [cadd(a, cmul(b, v)) for a, b, v in zip(at_t(cn, q), at_q(kl, q), c)]
            put_t(cn, q, c)
        return c

    first = lax.fori_loop(0, STEP // 4, back, [zero, zero])
    entering = []
    for h in range(2):
        v = first[h]
        for m, step in zip((1, 2, 4), hops[h]):
            v = cadd(v, cmul(step, later(v, m)))
        entering.append(cwhere(sub < SUB - 1, later(v, 1), zero))

    def fix(i, _):
        for u in range(4):
            q = 4 * i + u
            put_t(cn, q, [cadd(a, cmul(b, v)) for a, b, v in zip(at_t(cn, q), at_q(wq, q), entering)])
        return 0

    lax.fori_loop(0, STEP // 4, fix, 0)
    for h in range(2):
        gc[:, 256 * h : 256 * h + 256] = with_prev(cn, h)
    to_core = remote(gc.at[:, half(1 - core)], rcore, css.at[0], csr.at[0], sibling)
    to_core.start()
    to_core.wait_recv()
    gsum[...] = gc[:, half(core)] + rcore[...]
    to_x = scatter_x(gsum, rx, xss, xsr)
    for copy in to_q:
        copy.wait_recv()
    for copy in carries:
        copy.wait_recv()

    def pair(j, at):
        return bc[j, at : at + 2, :], bc[j, at + 2 : at + 4, :]

    zero2 = (jnp.zeros((2, 128), F32), jnp.zeros((2, 128), F32))
    one2 = (jnp.ones((2, 128), F32), jnp.zeros((2, 128), F32))
    chains = []
    for k in range(n_x):
        inside, passing, total, span = zero2, one2, zero2, one2
        for j in reversed(range(n_zl)):
            inside, passing = cwhere(j == zl, total, inside), cwhere(j == zl, span, passing)
            f, m = pair(k * n_zl + j, 0), pair(k * n_zl + j, 4)
            total, span = cadd(f, cmul(m, total)), cmul(m, span)
        chains.append((inside, passing, total, span))
    beyond, entry = zero2, zero2
    sums = [zero, zero]
    for j in reversed(range(n_x)):
        inside, passing, total, span = chains[j]
        here = cadd(inside, cmul(passing, beyond))
        entry = cwhere(j == x, here, entry)
        beyond = cadd(total, cmul(span, beyond))
        for h in range(2):
            e = (here[0][h : h + 1], here[1][h : h + 1])
            weight = (rq[j, :, 256 * h : 256 * h + 128], rq[j, :, 256 * h + 128 : 256 * h + 256])
            term = cmul(e, weight)
            sums[h] = term if j == n_x - 1 else cadd(sums[h], term)
    for h in range(2):
        for part in range(2):
            at = 256 * h + 128 * part
            eq[:, at : at + 128] = sums[h][part]
    to_core_2 = remote(eq.at[:, half(1 - core)], req, css.at[1], csr.at[1], sibling)
    to_core_2.start()
    for copy in to_x:
        copy.wait_recv()
    owned = jnp.sum(rx[...], axis=0) + eq[:, half(core)]
    to_core_2.wait_recv()
    rz[z] = owned + req[...]
    to_z = [remote(rz.at[z], rz.at[z], zss.at[d], zsr.at[d], at_z(d)) for d in far_first(n_z)]
    for copy in to_z:
        copy.start()
    for h in range(2):
        e = (entry[0][h : h + 1], entry[1][h : h + 1])
        c = cadd((cn[2 * h], cn[2 * h + 1]), cmul(e, (un[2 * h], un[2 * h + 1])))
        hi, lo = split(jnp.concatenate(c, axis=1))
        adj = dot(hi, whi[h], NT) + dot(lo, whi[h], NT) + dot(hi, wlo[h], NT)
        gi[0, :, 256 * h : 256 * h + 256] = adj.astype(BF16)
    for copy in to_z:
        copy.wait_recv()
    hi, lo = split(jnp.sum(rz[...], axis=0))
    gr[slab(x), half(core)] = dot(hi, whi[core], NT) + dot(lo, whi[core], NT) + dot(hi, wlo[core], NT)
    mine = gr.at[slab(x), half(core)]
    back_x = []
    for i, d in enumerate(far_first(n_own)):
        where = at_x(d if d <= n_own // 2 else n_x - n_own + d)
        back_x.append(remote(mine, mine, xas.at[i], xar.at[i], where))
        back_x[-1].start()
    for copy in back_x:
        copy.wait_recv()
    ours = gr.at[:, half(core)]
    back_core = remote(ours, ours, css.at[2], csr.at[2], sibling)
    back_core.start()

    def finish(h):
        gt[pl.ds(4 * h, 4)] = gr[:, half(h)].T.reshape(4, BS, BS)

    finish(core)
    back_core.wait_recv()
    finish(1 - core)

    for copy in a2a + to_q + carries + [to_core] + to_x + [to_core_2] + to_z + back_x + [back_core]:
        copy.wait_send()


def store(gi, gt, gi_out, gt_out, sem):
    copies = [pltpu.make_async_copy(gi, gi_out, sem.at[0]), pltpu.make_async_copy(gt, gt_out, sem.at[1])]
    for copy in copies:
        copy.start()
    for copy in copies:
        copy.wait()


def body(sizes, *operands):
    n_zh, n_core, n_x, n_zl, n_y = sizes
    n_z = n_zh * n_zl
    slab = BS // n_x
    vmem, anywhere = pl.BlockSpec(memory_space=pltpu.VMEM), pl.BlockSpec(memory_space=pltpu.HBM)
    plane = pltpu.VMEM((4, TOK, 128), F32)
    dma = pltpu.SemaphoreType.DMA
    made = pl.pallas_call(
        functools.partial(kernel, sizes),
        out_shape=(
            jax.ShapeDtypeStruct((1, TOK, CH), BF16),
            jax.ShapeDtypeStruct((NB, BS, BS), F32),
        ),
        in_specs=[anywhere] * 6,
        out_specs=(vmem, vmem),
        scratch_shapes=[
            pltpu.VMEM((1, TOK), I32),
            pltpu.VMEM((NB, 32), I32),
            pltpu.VMEM((NB, 32), I32),
            pltpu.VMEM((NB, 4, BS), F32),
            pltpu.VMEM((TOK, CH), BF16),
            pltpu.VMEM((TOK, CH), BF16),
            pltpu.VMEM((2, 256, 256), BF16),
            pltpu.VMEM((2, 256, 256), BF16),
            plane, plane, plane, plane, plane,
            pltpu.VMEM((BS, CH), F32),
            pltpu.VMEM((n_x, slab, CH), F32),
            pltpu.VMEM((BS, CH), F32),
            pltpu.VMEM((BS, CH), F32),
            pltpu.VMEM((n_x * n_zl, 8, 128), F32),
            pltpu.VMEM((BS, 256), F32),
            pltpu.VMEM((BS, 256), F32),
            pltpu.VMEM((n_x, slab, 256), F32),
            pltpu.VMEM((slab, CH), F32),
            pltpu.VMEM((slab, 256), F32),
            pltpu.VMEM((n_z, slab, 256), F32),
            dma((6,)),
            dma((n_y,)), dma((n_y,)),
            dma((n_x,)), dma((n_x,)),
            dma((n_x * n_zl,)), dma((n_x * n_zl,)),
            dma((3,)), dma((3,)),
            dma((n_x,)), dma((n_x,)),
            dma((n_z,)), dma((n_z,)),
            dma((n_x,)), dma((n_x,)),
            pltpu.SemaphoreType.REGULAR,
        ],
        compiler_params=pltpu.CompilerParams(
            collective_id=0, has_side_effects=True, vmem_limit_bytes=32 * 2**20
        ),
    )(*(pltpu.with_memory_space_constraint(a, pltpu.HBM) for a in operands))
    return pl.pallas_call(
        store,
        out_shape=tuple(jax.ShapeDtypeStruct(a.shape, a.dtype) for a in made),
        in_specs=[vmem] * 2,
        out_specs=(anywhere, anywhere),
        scratch_shapes=[dma((2,))],
        compiler_params=pltpu.CompilerParams(vmem_limit_bytes=16 * 2**20),
    )(*made)


def solution(mesh):
    n_dp, n_ctx, n_y = (mesh.shape[a] for a in ("dp", "ctx", "tensor"))
    n_x = min(8, n_ctx // 2)
    sizes = (n_dp // 2, 2, n_x, n_ctx // n_x, n_y)
    fine = Mesh(mesh.devices.reshape(sizes), ("zh", "core", "x", "zl", "y"))
    in_specs = (
        P(DP, (*CTX, "y"), None),
        P(DP, CTX, "y"),
        P(DP, CTX),
        P("y", None),
        P("y", None),
        P("y", None, None),
    )
    out_specs = (P(DP, CTX, "y"), P("y", None, None))
    return jax.shard_map(
        functools.partial(body, sizes), mesh=fine, in_specs=in_specs, out_specs=out_specs, check_vma=False
    )
```

```python
import functools
import math

import jax
import jax.numpy as jnp
from jax import lax
from jax.experimental import pallas as pl
from jax.experimental.pallas import tpu as pltpu
from jax.sharding import Mesh
from jax.sharding import PartitionSpec as P

F32, BF16, I32 = jnp.float32, jnp.bfloat16, jnp.int32
NN = (((1,), (0,)), ((), ()))
NT = (((1,), (1,)), ((), ()))
TN = (((0,), (0,)), ((), ()))
MESH = pl.DeviceIdType.MESH

TOK, CH, SUB, STEP = 256, 512, 8, 32
BS, NB = 64, 8
DP = ("zh", "core")
CTX = ("x", "zl")


def iota(shape, axis):
    return lax.broadcasted_iota(I32, shape, axis)


def dot(a, b, dims):
    return lax.dot_general(a, b, dims, preferred_element_type=F32)


def fdot(a, b, dims):
    return lax.dot_general(a, b, dims, precision=lax.Precision.HIGHEST, preferred_element_type=F32)


def split(a):
    hi = a.astype(BF16)
    return hi, (a - hi.astype(F32)).astype(BF16)


def cmul(a, b):
    return a[0] * b[0] - a[1] * b[1], a[0] * b[1] + a[1] * b[0]


def cadd(a, b):
    return a[0] + b[0], a[1] + b[1]


def cwhere(m, a, b):
    return jnp.where(m, a[0], b[0]), jnp.where(m, a[1], b[1])


def far_first(count):
    return sorted(range(1, count), key=lambda d: -min(d, count - d))


def compact(full):
    lane_block = (iota((BS, 256), 1) % 128) // 32
    out = jnp.zeros((BS, 256), F32)
    for bb in range(4):
        out = jnp.where(lane_block == bb, full[BS * bb : BS * bb + BS], out)
    return out


def kernel(
    sizes, og, ps, bd_in, ac_in, rc_in, rf_in, gi, gt,
    bd, ac, rc, rf, g, pv, whi, wlo, kl, wq, fw, un, cn, qc, rq, gc, gr, bc, ab, gsum, rcore, rx, eq, req, rz,
    lsem, ysend, yrecv, qss, qsr, bcs, bcr, css, csr, xss, xsr, zss, zsr, xas, xar, ready,
):
    n_zh, n_core, n_x, n_zl, n_y = sizes
    n_z = n_zh * n_zl
    zh, core, x, zl, y = (lax.axis_index(a) for a in ("zh", "core", "x", "zl", "y"))
    z = zh * n_zl + zl
    rows = TOK // n_y

    def at_y(d):
        return {"y": lax.rem(y + d, n_y)}

    def at_x(d):
        return {"x": lax.rem(x + d, n_x)}

    def at_z(d):
        k = lax.rem(z + d, n_z)
        return {"zh": k // n_zl, "zl": lax.rem(k, n_zl)}

    def at_ctx(d, e):
        return {"x": lax.rem(x + d, n_x), "zl": lax.rem(zl + e, n_zl)}

    sibling = {"core": 1 - core}
    partners = (
        [at_y(d) for d in far_first(n_y)]
        + [at_x(d) for d in far_first(n_x)]
        + [at_z(d) for d in far_first(n_z)]
        + [sibling]
    )
    barrier = pltpu.get_barrier_semaphore()
    for partner in partners:
        pl.semaphore_signal(barrier, inc=1, device_id=partner, device_id_type=MESH)

    def remote(src, dst, send, recv, where):
        return pltpu.make_async_remote_copy(
            src_ref=src, dst_ref=dst, send_sem=send, recv_sem=recv, device_id=where, device_id_type=MESH
        )

    small = [
        pltpu.make_async_copy(src, dst, lsem.at[2 + i])
        for i, (src, dst) in enumerate(((ac_in, ac), (rc_in, rc), (bd_in, bd), (rf_in, rf)))
    ]
    for copy in small:
        copy.start()
    load_prev = pltpu.make_async_copy(ps.at[0], pv, lsem.at[0])
    load_prev.start()
    own_rows = pl.ds(pl.multiple_of(y * rows, rows), rows)
    load_own = pltpu.make_async_copy(
        og.at[0, :, pl.ds(pl.multiple_of(y * CH, CH), CH)], g.at[own_rows], lsem.at[1]
    )
    load_own.start()
    for copy in small:
        copy.wait()
    pick = (iota((32, 128), 1) % 32 == iota((32, 128), 0)).astype(F32)
    acode = fdot(ac[...].astype(F32), pick, NN)
    rcode = fdot(rc[...].astype(F32), pick, NN)
    radius = 1.0 - jnp.exp2(-(4.0 + rcode * (10.0 / 1024.0)))
    angle = acode * (math.pi / 4096.0)
    lam_r, lam_i = radius * jnp.cos(angle), -radius * jnp.sin(angle)
    lam = []
    for h in range(2):
        mine = iota((NB, 128), 0) == 4 * h + iota((NB, 128), 1) // 32
        lam.append(
            tuple(
                jnp.broadcast_to(jnp.sum(jnp.where(mine, v, 0.0), axis=0, keepdims=True), (SUB, 128))
                for v in (lam_r, lam_i)
            )
        )

    r_id, t_id = iota((TOK, TOK), 0), iota((TOK, TOK), 1)
    chosen = t_id == (r_id % SUB) * STEP + r_id // SUB
    marks = jnp.where(chosen & (bd[...] == 1), 1.0, 0.0).astype(BF16)
    keep = jnp.where(dot(marks, jnp.ones((TOK, 128), BF16), NN) > 0.5, F32(0.6), F32(1.0))
    for h in range(2):
        for part in range(2):
            kl[2 * h + part] = keep * lam[h][part][0:1]

    pl.semaphore_wait(barrier, len(partners))
    for d in range(1, n_x):
        pl.semaphore_signal(ready, inc=1, device_id=at_x(d), device_id_type=MESH)

    a2a = []
    for d in range(1, n_y):
        k = lax.rem(y + d, n_y)
        a2a.append(
            remote(
                og.at[0, :, pl.ds(pl.multiple_of(k * CH, CH), CH)],
                g.at[own_rows], ysend.at[d], yrecv.at[d], {"y": k},
            )
        )
        a2a[-1].start()

    lane = iota((BS, 256), 1)
    spread = (iota((NB, 256), 1) // 32 == iota((NB, 256), 0)).astype(F32)
    xs = [(iota((BS, 256), 0) == 2 * (lane % 32) + part).astype(F32) for part in range(2)]
    for k in (3, 2, 1, 0):
        v = fdot(rf[:, k, :], spread, TN)
        scale = 2.0 / jnp.sum(v * v, axis=0, keepdims=True)
        xs = [m - v * (scale * jnp.sum(v * m, axis=0, keepdims=True)) for m in xs]
    lane_block = (lane % 128) // 32
    for h in range(2):
        half = jnp.concatenate([m[:, 128 * h : 128 * h + 128] for m in xs], axis=1)
        for bb in range(4):
            hi, lo = split(jnp.where(lane_block == bb, half, 0.0))
            whi[h, BS * bb : BS * bb + BS, :] = hi
            wlo[h, BS * bb : BS * bb + BS, :] = lo

    def at_q(ref, q):
        return [(ref[2 * h, pl.ds(q * SUB, SUB), :], ref[2 * h + 1, pl.ds(q * SUB, SUB), :]) for h in range(2)]

    def at_t(ref, q):
        return [
            (ref[2 * h, pl.ds(q, SUB, stride=STEP), :], ref[2 * h + 1, pl.ds(q, SUB, stride=STEP), :])
            for h in range(2)
        ]

    def put_t(ref, q, value):
        for h in range(2):
            for part in range(2):
                ref[2 * h + part, pl.ds(q, SUB, stride=STEP), :] = value[h][part]

    def weights(i, w):
        for u in range(4):
            q = STEP - 1 - (4 * i + u)
            w = [cmul(a, b) for a, b in zip(at_q(kl, q), w)]
            for h in range(2):
                for part in range(2):
                    wq[2 * h + part, pl.ds(q * SUB, SUB), :] = w[h][part]
        return w

    one = (jnp.ones((SUB, 128), F32), jnp.zeros((SUB, 128), F32))
    m1 = lax.fori_loop(0, STEP // 4, weights, [one, one])
    sub = iota((SUB, 128), 0)

    def later(v, m):
        return tuple(pltpu.roll(p, SUB - m, 0) for p in v)

    zero = (jnp.zeros((SUB, 128), F32), jnp.zeros((SUB, 128), F32))
    hops, base = [], []
    for h in range(2):
        steps = [cwhere(sub < SUB - 1, m1[h], zero)]
        b = cwhere(sub < SUB - 1, later(m1[h], 1), one)
        for m in (1, 2, 4):
            if m > 1:
                steps.append(cmul(steps[-1], later(steps[-1], m // 2)))
            b = cmul(b, cwhere(sub < SUB - m, later(b, m), one))
        hops.append(steps)
        base.append(b)

    def enter(i, _):
        for u in range(4):
            q = 4 * i + u
            put_t(un, q, [cmul(a, b) for a, b in zip(at_q(wq, q), base)])
        return 0

    lax.fori_loop(0, STEP // 4, enter, 0)

    def leave(i, w):
        for u in range(4):
            q = 4 * i + u
            put_t(fw, q, w)
            w = [cmul(a, b) for a, b in zip(at_q(kl, q), w)]
        return w

    lax.fori_loop(0, STEP // 4, leave, [one, one])
    mu = [(un[2 * h, 0:1, :], un[2 * h + 1, 0:1, :]) for h in range(2)]

    def half(k):
        return pl.ds(pl.multiple_of(k * 256, 256), 256)

    def with_prev(ref, h):
        prev = pv[:, half(h)]
        hi, lo = split(jnp.concatenate([ref[2 * h], ref[2 * h + 1]], axis=1))
        return compact(dot(prev, hi, TN) + dot(prev, lo, TN))

    n_own = n_x
    deep = BS // n_own

    def slab(k):
        return pl.ds(pl.multiple_of(lax.rem(k, n_own) * deep, deep), deep)

    def scatter_x(src, dst, send, recv):
        copies = []
        for d in far_first(n_x):
            k = lax.rem(x + d, n_x)
            copies.append(remote(src.at[slab(k)], dst.at[x], send.at[d], recv.at[d], {"x": k}))
            copies[-1].start()
        dst[x] = src[slab(x), :]
        return copies

    load_prev.wait()
    for h in range(2):
        qc[:, 256 * h : 256 * h + 256] = with_prev(un, h)
    to_q = scatter_x(qc, rq, qss, qsr)

    me = x * n_zl + zl
    for h in range(2):
        for part in range(2):
            bc[me, 4 + 2 * part + h : 5 + 2 * part + h, :] = mu[h][part]
    pl.semaphore_wait(ready, n_x - 1)
    offsets = [(d, e) for d in range(n_x) for e in range(n_zl) if d or e]
    offsets.sort(key=lambda o: -min(o[0], n_x - o[0]) - min(o[1], n_zl - o[1]))

    subs = rows // STEP

    def piece(k):
        at = pl.ds(pl.multiple_of(k * rows, rows), rows)
        for h in range(2):
            part = g[at, 256 * h : 256 * h + 256]
            turned = dot(part, whi[h], NN) + dot(part, wlo[h], NN)
            c = turned[:, :128], turned[:, 128:]
            cn[2 * h, at, :], cn[2 * h + 1, at, :] = c
            term = cmul((fw[2 * h, at, :], fw[2 * h + 1, at, :]), c)
            for i in range(2):
                ab[2 * h + i, pl.ds(k * subs, subs), :] = jnp.sum(term[i].reshape(subs, STEP, 128), axis=1)

    load_own.wait()
    piece(y)
    for d in reversed(far_first(n_y)):
        a2a[d - 1].wait_recv()
        piece(lax.rem(y + n_y - d, n_y))
    entering = []
    for h in range(2):
        v = (ab[2 * h], ab[2 * h + 1])
        for m, step in zip((1, 2, 4), hops[h]):
            v = cadd(v, cmul(step, later(v, m)))
        entering.append(cwhere(sub < SUB - 1, later(v, 1), zero))
        for part in range(2):
            bc[me, 2 * part + h : 2 * part + h + 1, :] = v[part][0:1]

    carries = [
        remote(bc.at[me], bc.at[me], bcs.at[i], bcr.at[i], at_ctx(*o)) for i, o in enumerate(offsets)
    ]
    for copy in carries:
        copy.start()

    def back(i, c):
        for u in range(4):
            q = STEP - 1 - (4 * i + u)
            c = [cadd(a, cmul(b, v)) for a, b, v in zip(at_t(cn, q), at_q(kl, q), c)]
            put_t(cn, q, c)
        return c

    lax.fori_loop(0, STEP // 4, back, entering)
    gc[:, half(1 - core)] = with_prev(cn, 1 - core)
    to_core = remote(gc.at[:, half(1 - core)], rcore, css.at[0], csr.at[0], sibling)
    to_core.start()
    gc[:, half(core)] = with_prev(cn, core)
    to_core.wait_recv()
    gsum[...] = gc[:, half(core)] + rcore[...]
    to_x = scatter_x(gsum, rx, xss, xsr)
    for copy in to_q:
        copy.wait_recv()
    for copy in carries:
        copy.wait_recv()

    def pair(j, at):
        return bc[j, at : at + 2, :], bc[j, at + 2 : at + 4, :]

    zero2 = (jnp.zeros((2, 128), F32), jnp.zeros((2, 128), F32))
    one2 = (jnp.ones((2, 128), F32), jnp.zeros((2, 128), F32))
    chains = []
    for k in range(n_x):
        inside, passing, total, span = zero2, one2, zero2, one2
        for j in reversed(range(n_zl)):
            inside, passing = cwhere(j == zl, total, inside), cwhere(j == zl, span, passing)
            f, m = pair(k * n_zl + j, 0), pair(k * n_zl + j, 4)
            total, span = cadd(f, cmul(m, total)), cmul(m, span)
        chains.append((inside, passing, total, span))
    beyond, entry = zero2, zero2
    sums = [zero, zero]
    for j in reversed(range(n_x)):
        inside, passing, total, span = chains[j]
        here = cadd(inside, cmul(passing, beyond))
        entry = cwhere(j == x, here, entry)
        beyond = cadd(total, cmul(span, beyond))
        for h in range(2):
            e = (here[0][h : h + 1], here[1][h : h + 1])
            weight = (rq[j, :, 256 * h : 256 * h + 128], rq[j, :, 256 * h + 128 : 256 * h + 256])
            term = cmul(e, weight)
            sums[h] = term if j == n_x - 1 else cadd(sums[h], term)
    for h in range(2):
        for part in range(2):
            at = 256 * h + 128 * part
            eq[:, at : at + 128] = sums[h][part]
    to_core_2 = remote(eq.at[:, half(1 - core)], req, css.at[1], csr.at[1], sibling)
    to_core_2.start()
    for copy in to_x:
        copy.wait_recv()
    owned = jnp.sum(rx[...], axis=0) + eq[:, half(core)]
    to_core_2.wait_recv()
    rz[z] = owned + req[...]
    to_z = [remote(rz.at[z], rz.at[z], zss.at[d], zsr.at[d], at_z(d)) for d in far_first(n_z)]
    for copy in to_z:
        copy.start()
    for h in range(2):
        e = (entry[0][h : h + 1], entry[1][h : h + 1])
        c = cadd((cn[2 * h], cn[2 * h + 1]), cmul(e, (un[2 * h], un[2 * h + 1])))
        hi, lo = split(jnp.concatenate(c, axis=1))
        adj = dot(hi, whi[h], NT) + dot(lo, whi[h], NT) + dot(hi, wlo[h], NT)
        gi[0, :, 256 * h : 256 * h + 256] = adj.astype(BF16)
    for copy in to_z:
        copy.wait_recv()
    hi, lo = split(jnp.sum(rz[...], axis=0))
    gr[slab(x), half(core)] = dot(hi, whi[core], NT) + dot(lo, whi[core], NT) + dot(hi, wlo[core], NT)
    mine = gr.at[slab(x), half(core)]
    back_x = []
    for i, d in enumerate(far_first(n_own)):
        where = at_x(d if d <= n_own // 2 else n_x - n_own + d)
        back_x.append(remote(mine, mine, xas.at[i], xar.at[i], where))
        back_x[-1].start()
    for copy in back_x:
        copy.wait_recv()
    ours = gr.at[:, half(core)]
    back_core = remote(ours, ours, css.at[2], csr.at[2], sibling)
    back_core.start()

    def finish(h):
        gt[pl.ds(4 * h, 4)] = gr[:, half(h)].T.reshape(4, BS, BS)

    finish(core)
    back_core.wait_recv()
    finish(1 - core)

    for copy in a2a + to_q  + carries + [to_core] + to_x + [to_core_2] + to_z + back_x + [back_core]:
        copy.wait_send()


def store(gi, gt, gi_out, gt_out, sem):
    copies = [pltpu.make_async_copy(gi, gi_out, sem.at[0]), pltpu.make_async_copy(gt, gt_out, sem.at[1])]
    for copy in copies:
        copy.start()
    for copy in copies:
        copy.wait()


def body(sizes, *operands):
    n_zh, n_core, n_x, n_zl, n_y = sizes
    n_z = n_zh * n_zl
    slab = BS // n_x
    vmem, anywhere = pl.BlockSpec(memory_space=pltpu.VMEM), pl.BlockSpec(memory_space=pltpu.HBM)
    plane = pltpu.VMEM((4, TOK, 128), F32)
    dma = pltpu.SemaphoreType.DMA
    made = pl.pallas_call(
        functools.partial(kernel, sizes),
        out_shape=(
            jax.ShapeDtypeStruct((1, TOK, CH), BF16),
            jax.ShapeDtypeStruct((NB, BS, BS), F32),
        ),
        in_specs=[anywhere] * 6,
        out_specs=(vmem, vmem),
        scratch_shapes=[
            pltpu.VMEM((1, TOK), I32),
            pltpu.VMEM((NB, 32), I32),
            pltpu.VMEM((NB, 32), I32),
            pltpu.VMEM((NB, 4, BS), F32),
            pltpu.VMEM((TOK, CH), BF16),
            pltpu.VMEM((TOK, CH), BF16),
            pltpu.VMEM((2, 256, 256), BF16),
            pltpu.VMEM((2, 256, 256), BF16),
            plane, plane, plane, plane, plane,
            pltpu.VMEM((BS, CH), F32),
            pltpu.VMEM((n_x, slab, CH), F32),
            pltpu.VMEM((BS, CH), F32),
            pltpu.VMEM((BS, CH), F32),
            pltpu.VMEM((n_x * n_zl, 8, 128), F32),
            pltpu.VMEM((4, SUB, 128), F32),
            pltpu.VMEM((BS, 256), F32),
            pltpu.VMEM((BS, 256), F32),
            pltpu.VMEM((n_x, slab, 256), F32),
            pltpu.VMEM((slab, CH), F32),
            pltpu.VMEM((slab, 256), F32),
            pltpu.VMEM((n_z, slab, 256), F32),
            dma((6,)),
            dma((n_y,)), dma((n_y,)),
            dma((n_x,)), dma((n_x,)),
            dma((n_x * n_zl,)), dma((n_x * n_zl,)),
            dma((3,)), dma((3,)),
            dma((n_x,)), dma((n_x,)),
            dma((n_z,)), dma((n_z,)),
            dma((n_x,)), dma((n_x,)),
            pltpu.SemaphoreType.REGULAR,
        ],
        compiler_params=pltpu.CompilerParams(
            collective_id=0, has_side_effects=True, vmem_limit_bytes=32 * 2**20
        ),
    )(*(pltpu.with_memory_space_constraint(a, pltpu.HBM) for a in operands))
    return pl.pallas_call(
        store,
        out_shape=tuple(jax.ShapeDtypeStruct(a.shape, a.dtype) for a in made),
        in_specs=[vmem] * 2,
        out_specs=(anywhere, anywhere),
        scratch_shapes=[dma((2,))],
        compiler_params=pltpu.CompilerParams(vmem_limit_bytes=16 * 2**20),
    )(*made)


def solution(mesh):
    n_dp, n_ctx, n_y = (mesh.shape[a] for a in ("dp", "ctx", "tensor"))
    n_x = min(8, n_ctx // 2)
    sizes = (n_dp // 2, 2, n_x, n_ctx // n_x, n_y)
    fine = Mesh(mesh.devices.reshape(sizes), ("zh", "core", "x", "zl", "y"))
    in_specs = (
        P(DP, (*CTX, "y"), None),
        P(DP, CTX, "y"),
        P(DP, CTX),
        P("y", None),
        P("y", None),
        P("y", None, None),
    )
    out_specs = (P(DP, CTX, "y"), P("y", None, None))
    return jax.shard_map(
        functools.partial(body, sizes), mesh=fine, in_specs=in_specs, out_specs=out_specs, check_vma=False
    )
```

```python
import functools
import math

import jax
import jax.numpy as jnp
from jax import lax
from jax.experimental import pallas as pl
from jax.experimental.pallas import tpu as pltpu
from jax.sharding import Mesh
from jax.sharding import PartitionSpec as P

F32, BF16, I32 = jnp.float32, jnp.bfloat16, jnp.int32
NN = (((1,), (0,)), ((), ()))
NT = (((1,), (1,)), ((), ()))
TN = (((0,), (0,)), ((), ()))
MESH = pl.DeviceIdType.MESH

TOK, CH, SUB, STEP = 256, 512, 8, 32
BS, NB = 64, 8
DP = ("zh", "core")
CTX = ("x", "zl")


def iota(shape, axis):
    return lax.broadcasted_iota(I32, shape, axis)


def dot(a, b, dims):
    return lax.dot_general(a, b, dims, preferred_element_type=F32)


def fdot(a, b, dims):
    return lax.dot_general(a, b, dims, precision=lax.Precision.HIGHEST, preferred_element_type=F32)


def split(a):
    hi = a.astype(BF16)
    return hi, (a - hi.astype(F32)).astype(BF16)


def cmul(a, b):
    return a[0] * b[0] - a[1] * b[1], a[0] * b[1] + a[1] * b[0]


def cadd(a, b):
    return a[0] + b[0], a[1] + b[1]


def cwhere(m, a, b):
    return jnp.where(m, a[0], b[0]), jnp.where(m, a[1], b[1])


def far_first(count):
    return sorted(range(1, count), key=lambda d: -min(d, count - d))


def compact(full):
    lane_block = (iota((BS, 256), 1) % 128) // 32
    out = jnp.zeros((BS, 256), F32)
    for bb in range(4):
        out = jnp.where(lane_block == bb, full[BS * bb : BS * bb + BS], out)
    return out


def kernel(
    sizes, og, ps, bd_in, ac_in, rc_in, rf_in, gi, gt,
    bd, ac, rc, rf, g, pv, whi, wlo, kl, wq, fw, un, cn, qc, rq, gc, gr, bc, ab, gsum, rcore, rx, eq, req, rz,
    lsem, ysend, yrecv, qss, qsr, bcs, bcr, css, csr, xss, xsr, zss, zsr, xas, xar, ready,
):
    n_zh, n_core, n_x, n_zl, n_y = sizes
    n_z = n_zh * n_zl
    zh, core, x, zl, y = (lax.axis_index(a) for a in ("zh", "core", "x", "zl", "y"))
    z = zh * n_zl + zl
    rows = TOK // n_y

    def at_y(d):
        return {"y": lax.rem(y + d, n_y)}

    def at_x(d):
        return {"x": lax.rem(x + d, n_x)}

    def at_z(d):
        k = lax.rem(z + d, n_z)
        return {"zh": k // n_zl, "zl": lax.rem(k, n_zl)}

    def at_ctx(d, e):
        return {"x": lax.rem(x + d, n_x), "zl": lax.rem(zl + e, n_zl)}

    sibling = {"core": 1 - core}
    partners = (
        [at_y(d) for d in far_first(n_y)]
        + [at_x(d) for d in far_first(n_x)]
        + [at_z(d) for d in far_first(n_z)]
        + [sibling]
    )
    barrier = pltpu.get_barrier_semaphore()
    for partner in partners:
        pl.semaphore_signal(barrier, inc=1, device_id=partner, device_id_type=MESH)

    def remote(src, dst, send, recv, where):
        return pltpu.make_async_remote_copy(
            src_ref=src, dst_ref=dst, send_sem=send, recv_sem=recv, device_id=where, device_id_type=MESH
        )

    small = [
        pltpu.make_async_copy(src, dst, lsem.at[2 + i])
        for i, (src, dst) in enumerate(((ac_in, ac), (rc_in, rc), (bd_in, bd), (rf_in, rf)))
    ]
    for copy in small:
        copy.start()
    load_prev = pltpu.make_async_copy(ps.at[0], pv, lsem.at[0])
    load_prev.start()
    own_rows = pl.ds(pl.multiple_of(y * rows, rows), rows)
    load_own = pltpu.make_async_copy(
        og.at[0, :, pl.ds(pl.multiple_of(y * CH, CH), CH)], g.at[own_rows], lsem.at[1]
    )
    load_own.start()
    for copy in small:
        copy.wait()
    pick = (iota((32, 128), 1) % 32 == iota((32, 128), 0)).astype(F32)
    acode = fdot(ac[...].astype(F32), pick, NN)
    rcode = fdot(rc[...].astype(F32), pick, NN)
    radius = 1.0 - jnp.exp2(-(4.0 + rcode * (10.0 / 1024.0)))
    angle = acode * (math.pi / 4096.0)
    lam_r, lam_i = radius * jnp.cos(angle), -radius * jnp.sin(angle)
    lam = []
    for h in range(2):
        mine = iota((NB, 128), 0) == 4 * h + iota((NB, 128), 1) // 32
        lam.append(
            tuple(
                jnp.broadcast_to(jnp.sum(jnp.where(mine, v, 0.0), axis=0, keepdims=True), (SUB, 128))
                for v in (lam_r, lam_i)
            )
        )

    r_id, t_id = iota((TOK, TOK), 0), iota((TOK, TOK), 1)
    chosen = t_id == (r_id % SUB) * STEP + r_id // SUB
    marks = jnp.where(chosen & (bd[...] == 1), 1.0, 0.0).astype(BF16)
    keep = jnp.where(dot(marks, jnp.ones((TOK, 128), BF16), NN) > 0.5, F32(0.6), F32(1.0))
    for h in range(2):
        for part in range(2):
            kl[2 * h + part] = keep * lam[h][part][0:1]

    pl.semaphore_wait(barrier, len(partners))
    for d in range(1, n_x):
        pl.semaphore_signal(ready, inc=1, device_id=at_x(d), device_id_type=MESH)

    a2a = []
    for d in range(1, n_y):
        k = lax.rem(y + d, n_y)
        a2a.append(
            remote(
                og.at[0, :, pl.ds(pl.multiple_of(k * CH, CH), CH)],
                g.at[own_rows], ysend.at[d], yrecv.at[d], {"y": k},
            )
        )
        a2a[-1].start()

    lane = iota((BS, 256), 1)
    spread = (iota((NB, 256), 1) // 32 == iota((NB, 256), 0)).astype(F32)
    xs = [(iota((BS, 256), 0) == 2 * (lane % 32) + part).astype(F32) for part in range(2)]
    for k in (3, 2, 1, 0):
        v = fdot(rf[:, k, :], spread, TN)
        scale = 2.0 / jnp.sum(v * v, axis=0, keepdims=True)
        xs = [m - v * (scale * jnp.sum(v * m, axis=0, keepdims=True)) for m in xs]
    lane_block = (lane % 128) // 32
    for h in range(2):
        half = jnp.concatenate([m[:, 128 * h : 128 * h + 128] for m in xs], axis=1)
        for bb in range(4):
            hi, lo = split(jnp.where(lane_block == bb, half, 0.0))
            whi[h, BS * bb : BS * bb + BS, :] = hi
            wlo[h, BS * bb : BS * bb + BS, :] = lo

    def at_q(ref, q):
        return [(ref[2 * h, pl.ds(q * SUB, SUB), :], ref[2 * h + 1, pl.ds(q * SUB, SUB), :]) for h in range(2)]

    def at_t(ref, q):
        return [
            (ref[2 * h, pl.ds(q, SUB, stride=STEP), :], ref[2 * h + 1, pl.ds(q, SUB, stride=STEP), :])
            for h in range(2)
        ]

    def put_t(ref, q, value):
        for h in range(2):
            for part in range(2):
                ref[2 * h + part, pl.ds(q, SUB, stride=STEP), :] = value[h][part]

    def weights(i, w):
        for u in range(4):
            q = STEP - 1 - (4 * i + u)
            w = [cmul(a, b) for a, b in zip(at_q(kl, q), w)]
            for h in range(2):
                for part in range(2):
                    wq[2 * h + part, pl.ds(q * SUB, SUB), :] = w[h][part]
        return w

    one = (jnp.ones((SUB, 128), F32), jnp.zeros((SUB, 128), F32))
    m1 = lax.fori_loop(0, STEP // 4, weights, [one, one])
    sub = iota((SUB, 128), 0)

    def later(v, m):
        return tuple(pltpu.roll(p, SUB - m, 0) for p in v)

    zero = (jnp.zeros((SUB, 128), F32), jnp.zeros((SUB, 128), F32))
    hops, base = [], []
    for h in range(2):
        steps = [cwhere(sub < SUB - 1, m1[h], zero)]
        b = cwhere(sub < SUB - 1, later(m1[h], 1), one)
        for m in (1, 2, 4):
            if m > 1:
                steps.append(cmul(steps[-1], later(steps[-1], m // 2)))
            b = cmul(b, cwhere(sub < SUB - m, later(b, m), one))
        hops.append(steps)
        base.append(b)

    def enter(i, _):
        for u in range(4):
            q = 4 * i + u
            put_t(un, q, [cmul(a, b) for a, b in zip(at_q(wq, q), base)])
        return 0

    lax.fori_loop(0, STEP // 4, enter, 0)

    def leave(i, w):
        for u in range(4):
            q = 4 * i + u
            put_t(fw, q, w)
            w = [cmul(a, b) for a, b in zip(at_q(kl, q), w)]
        return w

    lax.fori_loop(0, STEP // 4, leave, [one, one])
    mu = [(un[2 * h, 0:1, :], un[2 * h + 1, 0:1, :]) for h in range(2)]

    def half(k):
        return pl.ds(pl.multiple_of(k * 256, 256), 256)

    def with_prev(ref, h):
        prev = pv[:, half(h)]
        hi, lo = split(jnp.concatenate([ref[2 * h], ref[2 * h + 1]], axis=1))
        return compact(dot(prev, hi, TN) + dot(prev, lo, TN))

    n_own = n_x
    deep = BS // n_own

    def slab(k):
        return pl.ds(pl.multiple_of(lax.rem(k, n_own) * deep, deep), deep)

    def scatter_x(src, dst, send, recv):
        copies = []
        for d in far_first(n_x):
            k = lax.rem(x + d, n_x)
            copies.append(remote(src.at[slab(k)], dst.at[x], send.at[d], recv.at[d], {"x": k}))
            copies[-1].start()
        dst[x] = src[slab(x), :]
        return copies

    load_prev.wait()
    for h in range(2):
        qc[:, 256 * h : 256 * h + 256] = with_prev(un, h)
    to_q = scatter_x(qc, rq, qss, qsr)

    me = x * n_zl + zl
    for h in range(2):
        for part in range(2):
            bc[me, 4 + 2 * part + h : 5 + 2 * part + h, :] = mu[h][part]
    pl.semaphore_wait(ready, n_x - 1)
    offsets = [(d, e) for d in range(n_x) for e in range(n_zl) if d or e]
    offsets.sort(key=lambda o: -min(o[0], n_x - o[0]) - min(o[1], n_zl - o[1]))

    subs = rows // STEP

    def piece(k):
        at = pl.ds(pl.multiple_of(k * rows, rows), rows)
        for h in range(2):
            part = g[at, 256 * h : 256 * h + 256]
            turned = dot(part, whi[h], NN) + dot(part, wlo[h], NN)
            c = turned[:, :128], turned[:, 128:]
            cn[2 * h, at, :], cn[2 * h + 1, at, :] = c
            term = cmul((fw[2 * h, at, :], fw[2 * h + 1, at, :]), c)
            for i in range(2):
                ab[2 * h + i, pl.ds(k * subs, subs), :] = jnp.sum(term[i].reshape(subs, STEP, 128), axis=1)

    load_own.wait()
    piece(y)
    for d in reversed(far_first(n_y)):
        a2a[d - 1].wait_recv()
        piece(lax.rem(y + n_y - d, n_y))
    entering = []
    for h in range(2):
        v = (ab[2 * h], ab[2 * h + 1])
        for m, step in zip((1, 2, 4), hops[h]):
            v = cadd(v, cmul(step, later(v, m)))
        entering.append(cwhere(sub < SUB - 1, later(v, 1), zero))
        for part in range(2):
            bc[me, 2 * part + h : 2 * part + h + 1, :] = v[part][0:1]

    carries = [
        remote(bc.at[me], bc.at[me], bcs.at[i], bcr.at[i], at_ctx(*o)) for i, o in enumerate(offsets)
    ]
    for copy in carries:
        copy.start()

    def back(i, c):
        for u in range(4):
            q = STEP - 1 - (4 * i + u)
            c = [cadd(a, cmul(b, v)) for a, b, v in zip(at_t(cn, q), at_q(kl, q), c)]
            put_t(cn, q, c)
        return c

    lax.fori_loop(0, STEP // 4, back, entering)
    gc[:, half(1 - core)] = with_prev(cn, 1 - core)
    to_core = remote(gc.at[:, half(1 - core)], rcore, css.at[0], csr.at[0], sibling)
    to_core.start()
    gc[:, half(core)] = with_prev(cn, core)
    to_core.wait_recv()
    gsum[...] = gc[:, half(core)] + rcore[...]
    to_x = scatter_x(gsum, rx, xss, xsr)
    for copy in to_q:
        copy.wait_recv()
    for copy in carries:
        copy.wait_recv()

    def pair(j, at):
        return bc[j, at : at + 2, :], bc[j, at + 2 : at + 4, :]

    zero2 = (jnp.zeros((2, 128), F32), jnp.zeros((2, 128), F32))
    one2 = (jnp.ones((2, 128), F32), jnp.zeros((2, 128), F32))
    chains = []
    for k in range(n_x):
        inside, passing, total, span = zero2, one2, zero2, one2
        for j in reversed(range(n_zl)):
            inside, passing = cwhere(j == zl, total, inside), cwhere(j == zl, span, passing)
            f, m = pair(k * n_zl + j, 0), pair(k * n_zl + j, 4)
            total, span = cadd(f, cmul(m, total)), cmul(m, span)
        chains.append((inside, passing, total, span))
    beyond, entry = zero2, zero2
    sums = [zero, zero]
    for j in reversed(range(n_x)):
        inside, passing, total, span = chains[j]
        here = cadd(inside, cmul(passing, beyond))
        entry = cwhere(j == x, here, entry)
        beyond = cadd(total, cmul(span, beyond))
        for h in range(2):
            e = (here[0][h : h + 1], here[1][h : h + 1])
            weight = (rq[j, :, 256 * h : 256 * h + 128], rq[j, :, 256 * h + 128 : 256 * h + 256])
            term = cmul(e, weight)
            sums[h] = term if j == n_x - 1 else cadd(sums[h], term)
    for h in range(2):
        for part in range(2):
            at = 256 * h + 128 * part
            eq[:, at : at + 128] = sums[h][part]
    to_core_2 = remote(eq.at[:, half(1 - core)], req, css.at[1], csr.at[1], sibling)
    to_core_2.start()
    for copy in to_x:
        copy.wait_recv()
    owned = jnp.sum(rx[...], axis=0) + eq[:, half(core)]
    to_core_2.wait_recv()
    rz[z] = owned + req[...]
    to_z = [remote(rz.at[z], rz.at[z], zss.at[d], zsr.at[d], at_z(d)) for d in far_first(n_z)]
    for copy in to_z:
        copy.start()
    for h in range(2):
        e = (entry[0][h : h + 1], entry[1][h : h + 1])
        c = cadd((cn[2 * h], cn[2 * h + 1]), cmul(e, (un[2 * h], un[2 * h + 1])))
        hi, lo = split(jnp.concatenate(c, axis=1))
        adj = dot(hi, whi[h], NT) + dot(lo, whi[h], NT) + dot(hi, wlo[h], NT)
        gi[0, :, 256 * h : 256 * h + 256] = adj.astype(BF16)
    for copy in to_z:
        copy.wait_recv()
    hi, lo = split(jnp.sum(rz[...], axis=0))
    gr[slab(x), half(core)] = dot(hi, whi[core], NT) + dot(lo, whi[core], NT) + dot(hi, wlo[core], NT)
    mine = gr.at[slab(x), half(core)]
    back_x = []
    for i, d in enumerate(far_first(n_own)):
        where = at_x(d if d <= n_own // 2 else n_x - n_own + d)
        back_x.append(remote(mine, mine, xas.at[i], xar.at[i], where))
        back_x[-1].start()
    back_core = [remote(mine, mine, css.at[2], csr.at[2], sibling)]
    back_core[0].start()
    for i, d in reversed(list(enumerate(far_first(n_own)))):
        back_x[i].wait_recv()
        part = gr.at[slab(lax.rem(x + n_x - d, n_x)), half(core)]
        back_core.append(remote(part, part, css.at[3 + i], csr.at[3 + i], sibling))
        back_core[-1].start()

    def finish(h):
        gt[pl.ds(4 * h, 4)] = gr[:, half(h)].T.reshape(4, BS, BS)

    finish(core)
    for copy in back_core:
        copy.wait_recv()
    finish(1 - core)

    for copy in a2a + to_q  + carries + [to_core] + to_x + [to_core_2] + to_z + back_x + back_core:
        copy.wait_send()


def store(gi, gt, gi_out, gt_out, sem):
    copies = [pltpu.make_async_copy(gi, gi_out, sem.at[0]), pltpu.make_async_copy(gt, gt_out, sem.at[1])]
    for copy in copies:
        copy.start()
    for copy in copies:
        copy.wait()


def body(sizes, *operands):
    n_zh, n_core, n_x, n_zl, n_y = sizes
    n_z = n_zh * n_zl
    slab = BS // n_x
    vmem, anywhere = pl.BlockSpec(memory_space=pltpu.VMEM), pl.BlockSpec(memory_space=pltpu.HBM)
    plane = pltpu.VMEM((4, TOK, 128), F32)
    dma = pltpu.SemaphoreType.DMA
    made = pl.pallas_call(
        functools.partial(kernel, sizes),
        out_shape=(
            jax.ShapeDtypeStruct((1, TOK, CH), BF16),
            jax.ShapeDtypeStruct((NB, BS, BS), F32),
        ),
        in_specs=[anywhere] * 6,
        out_specs=(vmem, vmem),
        scratch_shapes=[
            pltpu.VMEM((1, TOK), I32),
            pltpu.VMEM((NB, 32), I32),
            pltpu.VMEM((NB, 32), I32),
            pltpu.VMEM((NB, 4, BS), F32),
            pltpu.VMEM((TOK, CH), BF16),
            pltpu.VMEM((TOK, CH), BF16),
            pltpu.VMEM((2, 256, 256), BF16),
            pltpu.VMEM((2, 256, 256), BF16),
            plane, plane, plane, plane, plane,
            pltpu.VMEM((BS, CH), F32),
            pltpu.VMEM((n_x, slab, CH), F32),
            pltpu.VMEM((BS, CH), F32),
            pltpu.VMEM((BS, CH), F32),
            pltpu.VMEM((n_x * n_zl, 8, 128), F32),
            pltpu.VMEM((4, SUB, 128), F32),
            pltpu.VMEM((BS, 256), F32),
            pltpu.VMEM((BS, 256), F32),
            pltpu.VMEM((n_x, slab, 256), F32),
            pltpu.VMEM((slab, CH), F32),
            pltpu.VMEM((slab, 256), F32),
            pltpu.VMEM((n_z, slab, 256), F32),
            dma((6,)),
            dma((n_y,)), dma((n_y,)),
            dma((n_x,)), dma((n_x,)),
            dma((n_x * n_zl,)), dma((n_x * n_zl,)),
            dma((3 + n_x,)), dma((3 + n_x,)),
            dma((n_x,)), dma((n_x,)),
            dma((n_z,)), dma((n_z,)),
            dma((n_x,)), dma((n_x,)),
            pltpu.SemaphoreType.REGULAR,
        ],
        compiler_params=pltpu.CompilerParams(
            collective_id=0, has_side_effects=True, vmem_limit_bytes=32 * 2**20
        ),
    )(*(pltpu.with_memory_space_constraint(a, pltpu.HBM) for a in operands))
    return pl.pallas_call(
        store,
        out_shape=tuple(jax.ShapeDtypeStruct(a.shape, a.dtype) for a in made),
        in_specs=[vmem] * 2,
        out_specs=(anywhere, anywhere),
        scratch_shapes=[dma((2,))],
        compiler_params=pltpu.CompilerParams(vmem_limit_bytes=16 * 2**20),
    )(*made)


def solution(mesh):
    n_dp, n_ctx, n_y = (mesh.shape[a] for a in ("dp", "ctx", "tensor"))
    n_x = min(8, n_ctx // 2)
    sizes = (n_dp // 2, 2, n_x, n_ctx // n_x, n_y)
    fine = Mesh(mesh.devices.reshape(sizes), ("zh", "core", "x", "zl", "y"))
    in_specs = (
        P(DP, (*CTX, "y"), None),
        P(DP, CTX, "y"),
        P(DP, CTX),
        P("y", None),
        P("y", None),
        P("y", None, None),
    )
    out_specs = (P(DP, CTX, "y"), P("y", None, None))
    return jax.shard_map(
        functools.partial(body, sizes), mesh=fine, in_specs=in_specs, out_specs=out_specs, check_vma=False
    )
```
